256 devices in a mesh: row: 16 (over z, core), grid: 16 (over x, y).
Axes of the slice: x: 4, y: 4, z: 8, core: 2. Of those that a mesh axis runs over, the one named last changes fastest.
Arguments:
- right_side: float32 [64, 32, 192, 256], P('row', 'grid'), may hold values from -6 to 6
- fine_blocks: bfloat16 [64, 32, 6, 192, 192], P('row', 'grid')
- fine_columns: int32 [64, 32, 6], P('row', 'grid'), may hold values from 0 to 8, as said below
- fine_prolong: bfloat16 [64, 32, 2, 192, 192], P('row', 'grid'), may hold values from -0.21875 to 0.21875
- fine_targets: int32 [64, 32, 2], P('row', 'grid'), may hold values from 0 to 7
- middle_blocks: bfloat16 [128, 3, 192, 192], P('row')
- middle_columns: int32 [128, 3], P('row'), may hold values from 0 to 2, as said below
- middle_prolong: bfloat16 [128, 2, 192, 192], P('row'), may hold values from -0.21875 to 0.21875
- middle_targets: int32 [128, 2], P('row'), may hold values from 0 to 3
Outputs:
- smooth_fine: float32 [64, 32, 192, 256], P('row', 'grid')
- smooth_middle: float32 [128, 192, 256], P('row')
- coarsest_right: float32 [4, 192, 256], replicated
The draws below stay inside these ranges and needn't reach their ends.
Inputs may be any that keep to these rules, and one draw needn't show every extreme that they name: `fine_columns`: slot 0 of every block row is 4, its own block; entries of other slots may repeat. `middle_columns`: slot 0 of every block row is 1, its own block. In each aligned group of 8 block rows, slot 1 of the first row is 0 and slot 2 of the last row is 2; entries of other slots may repeat.
All inputs are finite; a program needn't handle non-finite values.
Results may differ from the reference program's by a relative error of at most 0.033.
Values may be sent and summed in bfloat16 or wider, within the bound.
A program may use at most 128 MiB of HBM per device.

```python
from functools import partial
import jax
import jax.numpy as jnp
from jax import lax

BS = 192
LOADS = 256
RBX = 4
C2_DEV = 8
C3 = 4
K = 6
KP = 2
K2 = 3
KP2 = 2
DEG = 3
BX = 64
BY = 32
C2 = 128
N_ROW = 16


def block_values(key, shape, spread):
    noise_part = jnp.clip(jax.random.normal(key, shape, jnp.float32), -5.0, 5.0) * spread
    last_axis = len(shape) - 1
    slot_index = lax.broadcasted_iota(jnp.int32, shape, last_axis - 2)
    on_diagonal = lax.broadcasted_iota(jnp.int32, shape, last_axis - 1) == lax.broadcasted_iota(jnp.int32, shape, last_axis)
    shifted = jnp.where((slot_index == 0) & on_diagonal, 2.0, 0.0)
    return (noise_part + shifted).astype(jnp.bfloat16)


def draw_fine_blocks(key, part):
    return block_values(key, (BX, BY, K, BS, BS), 0.28 / BS ** 0.5)


def draw_middle_blocks(key, part):
    return block_values(key, (C2, K2, BS, BS), 0.4 / BS ** 0.5)


def draw_fine_columns(key, part):
    picks = jax.random.randint(key, (BX, BY, K), 0, 9, jnp.int32)
    slot_index = lax.broadcasted_iota(jnp.int32, (BX, BY, K), 2)
    return jnp.where(slot_index == 0, 4, picks).astype(jnp.int32)


def draw_middle_columns(key, part):
    picks = jax.random.randint(key, (C2, K2), 0, 3, jnp.int32)
    slot_index = lax.broadcasted_iota(jnp.int32, (C2, K2), 1)
    row_index = lax.broadcasted_iota(jnp.int32, (C2, K2), 0)
    within = row_index % C2_DEV
    picks = jnp.where((within == 0) & (slot_index == 1), 0, picks)
    picks = jnp.where((within == C2_DEV - 1) & (slot_index == 2), 2, picks)
    return jnp.where(slot_index == 0, 1, picks).astype(jnp.int32)


def set_ends(result, own_key, smallest, top_value):
    shape = result.shape
    place = [jax.random.randint(jax.random.fold_in(own_key, axis), (), 0, shape[axis]) for axis in range(len(shape))]
    result = result.at[tuple(place)].set(smallest)
    longest = shape.index(max(shape))
    place[longest] = (place[longest] + 1) % shape[longest]
    return result.at[tuple(place)].set(top_value)


def block_scale(own_key, dims, cuts, smallest, top_value):
    level, own = 1.0, jax.random.fold_in(own_key, 6)
    for dim, blocks in cuts:
        draws = jnp.exp(jax.random.uniform(jax.random.fold_in(own, dim), (blocks,), jnp.float32, smallest / len(cuts), top_value / len(cuts)))
        level = level * jnp.repeat(draws, dims[dim] // blocks).reshape([-1 if axis == dim else 1 for axis in range(len(dims))])
    return level


def bell_draw(stream_key, extent, scale, limit, shards=(), kind=jnp.bfloat16):
    array = scale * jax.random.normal(stream_key, extent, jnp.float32)
    if shards:
        array = array * block_scale(stream_key, extent, shards, -0.22, 0.18)
    return jnp.clip(array, -limit, limit).astype(kind)


def setup_inputs(seed: int = 0) -> dict:
    splits = jax.random.split(jax.random.key(seed), 10)
    right_side = bell_draw(splits[0], (BX, BY, BS, LOADS), 1.0, 6.0, ((0, 16), (1, 16)), jnp.float32)
    fine_blocks = draw_fine_blocks(jax.random.fold_in(splits[9], 71), 0)
    fine_columns = draw_fine_columns(jax.random.fold_in(splits[9], 71), 0)
    fine_prolong = bell_draw(splits[3], (BX, BY, KP, BS, BS), (4 * BS) ** -0.5, 0.21875, ((0, 16), (1, 16)))
    fine_targets = set_ends(jax.random.randint(splits[4], (BX, BY, KP), 0, C2_DEV), jax.random.fold_in(splits[4], 1), 0, C2_DEV - 1).astype(jnp.int32)
    middle_blocks = draw_middle_blocks(jax.random.fold_in(splits[9], 71), 0)
    middle_columns = draw_middle_columns(jax.random.fold_in(splits[9], 71), 0)
    middle_prolong = bell_draw(splits[7], (C2, KP2, BS, BS), (4 * BS) ** -0.5, 0.21875, ((0, 16),))
    middle_targets = set_ends(jax.random.randint(splits[8], (C2, KP2), 0, C3), jax.random.fold_in(splits[8], 1), 0, C3 - 1).astype(jnp.int32)
    return {"right_side": right_side, "fine_blocks": fine_blocks, "fine_columns": fine_columns, "fine_prolong": fine_prolong, "fine_targets": fine_targets, "middle_blocks": middle_blocks, "middle_columns": middle_columns, "middle_prolong": middle_prolong, "middle_targets": middle_targets}


cheb_low = 0.6
cheb_high = 6.0


def chebyshev(apply_operator, right_part):
    central_value = 0.5 * (cheb_high + cheb_low)
    half_width = 0.5 * (cheb_high - cheb_low)
    ratio_value = central_value / half_width
    rho_old = 1.0 / ratio_value
    direction = right_part / central_value
    iterate = direction
    residual = right_part
    for sweep_index in range(DEG):
        rounded = lax.optimization_barrier(direction.astype(jnp.bfloat16))
        residual = residual - apply_operator(rounded)
        if sweep_index + 1 < DEG:
            rho_new = 1.0 / (2.0 * ratio_value - rho_old)
            direction = (rho_new * rho_old) * direction + (2.0 * rho_new / half_width) * residual
            iterate = iterate + direction
            rho_old = rho_new
    return iterate, residual


def fine_apply(block_matrices, columns, vector):
    padded_input = jnp.pad(vector, ((1, 1), (1, 1), (0, 0), (0, 0)))
    offset_cols = jnp.arange(BY, dtype=jnp.int32)

    def one_row(index):
        row_columns = columns[index]
        row_pick = index + row_columns // 3
        col_pick = offset_cols[:, None] + row_columns % 3
        picked = padded_input[row_pick, col_pick].astype(jnp.float32)
        return jnp.einsum("ykab,ykbn->yan", block_matrices[index].astype(jnp.float32), picked)

    return lax.map(one_row, jnp.arange(BX, dtype=jnp.int32))


def middle_apply(block_matrices, columns, vector):
    padded_input = jnp.pad(vector, ((1, 1), (0, 0), (0, 0)))
    position = jnp.arange(C2, dtype=jnp.int32)[:, None] + columns
    picked = padded_input[position].astype(jnp.float32)
    return jnp.einsum("ikab,ikbn->ian", block_matrices.astype(jnp.float32), picked)


def restrict_fine(prolongation, targets, residual):
    rounded = lax.optimization_barrier(residual.astype(jnp.bfloat16))

    def one_group(group):
        start = group * RBX
        group_prolong = lax.dynamic_slice_in_dim(prolongation, start, RBX, 0).astype(jnp.float32)
        group_targets = lax.dynamic_slice_in_dim(targets, start, RBX, 0)
        group_residual = lax.dynamic_slice_in_dim(rounded, start, RBX, 0).astype(jnp.float32)
        pieces = jnp.einsum("xykab,xyan->xykbn", group_prolong, group_residual)
        return jax.ops.segment_sum(pieces.reshape(-1, BS, LOADS), group_targets.reshape(-1), num_segments=C2_DEV)

    summed = lax.map(one_group, jnp.arange(N_ROW, dtype=jnp.int32))
    return summed.reshape(C2, BS, LOADS)


def reference(right_side, fine_blocks, fine_columns, fine_prolong, fine_targets, middle_blocks, middle_columns, middle_prolong, middle_targets):
    smooth_fine, fine_residual = chebyshev(partial(fine_apply, fine_blocks, fine_columns), right_side)
    middle_right = restrict_fine(fine_prolong, fine_targets, fine_residual)
    smooth_middle, middle_residual = chebyshev(partial(middle_apply, middle_blocks, middle_columns), middle_right)
    middle_rounded = lax.optimization_barrier(middle_residual.astype(jnp.bfloat16)).astype(jnp.float32)
    pieces = jnp.einsum("ikab,ian->ikbn", middle_prolong.astype(jnp.float32), middle_rounded)
    coarsest_right = jax.ops.segment_sum(pieces.reshape(-1, BS, LOADS), middle_targets.reshape(-1), num_segments=C3)
    return smooth_fine, smooth_middle, coarsest_right
```

```python
import functools

import jax
import jax.numpy as jnp
from jax import lax
from jax.experimental import pallas as pl
from jax.experimental.pallas import tpu as pltpu
from jax.sharding import PartitionSpec as P

MESH = pl.DeviceIdType.MESH
F32 = jnp.float32
BF16 = jnp.bfloat16

C3 = 4
DEG = 3
PARTS = 2

cheb_low = 0.6
cheb_high = 6.0
CENTRE = 0.5 * (cheb_high + cheb_low)
HALF = 0.5 * (cheb_high - cheb_low)


def sweep_factors():
    ratio = CENTRE / HALF
    rho = 1.0 / ratio
    factors = []
    for _ in range(DEG - 1):
        rho_next = 1.0 / (2.0 * ratio - rho)
        factors.append((rho_next * rho, 2.0 * rho_next / HALF))
        rho = rho_next
    return factors


def copy_to(src, dst, send, recv, row, grid):
    return pltpu.make_async_remote_copy(
        src_ref=src, dst_ref=dst, send_sem=send, recv_sem=recv, device_id=(row, grid), device_id_type=MESH
    )


def kernel(
    n_row, n_grid,
    b_hbm, fb_hbm, fc, fp_hbm, ft, mb_hbm, mc, mp_hbm, mt,
    out_f, out_m, out_c,
    res, dirn, itr, fb, fp, mb, mp, halos, pieces, rs_send, rs_recv,
    m_halos, m_res, m_dir, m_itr, ag_send, ag_recv, m_turn, m_out,
    c_pair_send, c_pair_recv, c_z_send, c_z_recv, c_g_send, c_g_recv, c_all, c_turn, c_out,
    in_sem, out_sem, w_sem,
    g_send, g_recv, r_send, r_recv, k_send, k_recv,
    rs_ssem, rs_rsem, mh_send, mh_recv, ag_ssem, ag_rsem,
    cp_ssem, cp_rsem, cz_ssem, cz_rsem, cg_ssem, cg_rsem, ca_ssem, ca_rsem,
):
    r = lax.axis_index("row")
    g = lax.axis_index("grid")
    rx, ry = res.shape[0], res.shape[1]
    bs, loads = res.shape[2], res.shape[3]
    width = loads // PARTS
    lpd = width // n_grid
    LPD = lpd * PARTS
    n_mid = mb.shape[0]
    n_pair = n_row // 2
    core = lax.rem(r, 2)
    mate = r + 1 - 2 * core
    top, bottom = r == 0, r == n_row - 1
    first, last = g == 0, g == n_grid - 1
    half_c = C3 // 2

    for x in range(rx):
        pltpu.make_async_copy(b_hbm.at[x], res.at[x], in_sem.at[x]).start()
    weights = (
        pltpu.make_async_copy(fb_hbm, fb, w_sem.at[0]),
        pltpu.make_async_copy(fp_hbm, fp, w_sem.at[1]),
        pltpu.make_async_copy(mb_hbm, mb, w_sem.at[2]),
        pltpu.make_async_copy(mp_hbm, mp, w_sem.at[3]),
    )
    for w in weights:
        w.start()

    barrier = pltpu.get_barrier_semaphore()

    def greet(row, grid):
        pl.semaphore_signal(barrier, inc=1, device_id=(row, grid), device_id_type=MESH)

    @pl.loop(1, n_grid)
    def _(s):
        greet(r, lax.rem(g + s, n_grid))

    @pl.loop(1, n_pair)
    def _(s):
        greet(lax.rem(r + 2 * s, n_row), g)

    greet(mate, g)
    outer = r - 1 + 2 * core
    has_outer = jnp.logical_and(outer >= 0, outer < n_row)

    @pl.when(has_outer)
    def _():
        greet(outer, g)

    zero = jnp.zeros((bs, width), BF16)

    def clear_row(xi):
        for it in range(DEG):
            for h in range(PARTS):
                for yi in range(ry + 2):
                    halos[it][h][yi, xi] = zero

    def clear_column(yi):
        for it in range(DEG):
            for h in range(PARTS):
                for xi in range(rx + 2):
                    halos[it][h][yi, xi] = zero

    @pl.when(top)
    def _():
        clear_row(0)
        for it in range(DEG):
            m_halos[it][0] = jnp.zeros((LPD, bs), BF16)

    @pl.when(bottom)
    def _():
        clear_row(rx + 1)
        for it in range(DEG):
            m_halos[it][n_mid + 1] = jnp.zeros((LPD, bs), BF16)

    @pl.when(first)
    def _():
        clear_column(0)

    @pl.when(last)
    def _():
        clear_column(ry + 1)

    def send_block(it, h, x, y):
        src = halos[it][h].at[y + 1, x + 1]
        to = g + 2 * y - 1

        @pl.when(jnp.logical_and(to >= 0, to < n_grid))
        def _():
            dst = halos[it][h].at[3 * (1 - y), x + 1]
            copy_to(src, dst, g_send.at[it, h, y, x], g_recv.at[it, h, 1 - y, x], r, to).start()

        @pl.when(jnp.logical_and(x == 0, jnp.logical_not(top)))
        def _():
            dst = halos[it][h].at[y + 1, rx + 1]
            copy_to(src, dst, r_send.at[it, h, 0, y], r_recv.at[it, h, 1, y], r - 1, g).start()

        @pl.when(jnp.logical_and(x == rx - 1, jnp.logical_not(bottom)))
        def _():
            dst = halos[it][h].at[y + 1, 0]
            copy_to(src, dst, r_send.at[it, h, 1, y], r_recv.at[it, h, 0, y], r + 1, g).start()

    def grid_block(it, h, side, x):
        block = halos[it][h].at[3 * side, x + 1]
        return copy_to(block, block, g_send.at[it, h, 1 - side, x], g_recv.at[it, h, side, x], r, g)

    def corner(it, h, up, side):
        src = halos[it][h].at[3 * side, 1 + up * (rx - 1)]
        dst = halos[it][h].at[3 * side, (rx + 1) * (1 - up)]
        return copy_to(src, dst, k_send.at[it, h, up, side], k_recv.at[it, h, 1 - up, side], r - 1 + 2 * up, g)

    def row_block(it, h, up, y):
        block = halos[it][h].at[y + 1, (rx + 1) * up]
        return copy_to(block, block, r_send.at[it, h, up, y], r_recv.at[it, h, up, y], r, g)

    def corner_in(it, h, up, side):
        block = halos[it][h].at[3 * side, (rx + 1) * up]
        return copy_to(block, block, k_send.at[it, h, up, side], k_recv.at[it, h, up, side], r, g)

    sides = ((0, jnp.logical_not(first)), (1, jnp.logical_not(last)))
    ends = ((0, jnp.logical_not(top)), (1, jnp.logical_not(bottom)))

    def forward_corners(it, h):
        for side, there in sides:
            @pl.when(there)
            def _():
                for up, on in ends:
                    grid_block(it, h, side, up * (rx - 1)).wait_recv()

                    @pl.when(on)
                    def _():
                        corner(it, h, up, side).start()

    def wait_halo(it, h):
        for side, there in sides:
            @pl.when(there)
            def _():
                for x in range(1, rx - 1):
                    grid_block(it, h, side, x).wait_recv()
        for up, on in ends:
            @pl.when(on)
            def _():
                for y in range(ry):
                    row_block(it, h, up, y).wait_recv()
                for side, there in sides:
                    @pl.when(there)
                    def _():
                        corner_in(it, h, up, side).wait_recv()

    def order(t):
        return lax.rem(rx - 1 - lax.div(t, ry) + 1, rx), lax.rem(t, ry)

    for x in range(rx):
        pltpu.make_async_copy(b_hbm.at[x], res.at[x], in_sem.at[x]).wait()
    for h in range(PARTS):
        cols = slice(h * width, (h + 1) * width)

        @pl.loop(0, rx * ry)
        def _(t):
            x, y = order(t)
            start = res[x, y, :, cols] * (1.0 / CENTRE)
            halos[0][h][y + 1, x + 1] = start.astype(BF16)
            if h == 0:
                @pl.when(t == 0)
                def _():
                    pl.semaphore_wait(barrier, n_grid - 1 + n_pair + jnp.where(has_outer, 1, 0))
            send_block(0, h, x, y)
            dirn[x, y, :, cols] = start

    weights[0].wait()
    weights[1].wait()
    factors = sweep_factors()
    n_pieces = pieces.shape[0]
    kp = fp.shape[2]

    for it in range(DEG):
        for h in range(PARTS):
            cols = slice(h * width, (h + 1) * width)
            forward_corners(it, h)
            wait_halo(it, h)

            @pl.loop(0, rx * ry)
            def _(t):
                x, y = order(t)
                total = None
                for k in range(fb.shape[2]):
                    c = fc[x, y, k]
                    cx = lax.shift_right_logical(c * 11, 5)
                    picked = halos[it][h][y + c - 3 * cx, x + cx]
                    term = jnp.dot(fb[x, y, k], picked, preferred_element_type=F32)
                    total = term if total is None else total + term
                left = res[x, y, :, cols] - total
                if it < DEG - 1:
                    res[x, y, :, cols] = left
                    alpha, beta = factors[it]
                    old = dirn[x, y, :, cols]
                    new = alpha * old + beta * left
                    halos[it + 1][h][y + 1, x + 1] = new.astype(BF16)
                    send_block(it + 1, h, x, y)
                    if it == 0:
                        dirn[x, y, :, cols] = new
                        itr[x, y, :, cols] = old + new
                    else:
                        itr[x, y, :, cols] = itr[x, y, :, cols] + new
                else:
                    turned = left.astype(BF16).T
                    for k in range(kp):
                        pieces[(x * ry + y) * kp + k] = jnp.dot(turned, fp[x, y, k], preferred_element_type=F32)

            if it == DEG - 2 and h == PARTS - 1:
                pltpu.make_async_copy(itr, out_f, out_sem.at[0]).start()

            if it == DEG - 1:
                def one_share(to):
                    rows = pl.ds(pl.multiple_of(to * lpd, lpd), lpd)
                    sums = [None] * n_mid
                    for p in range(n_pieces):
                        piece = pieces[p, rows, :]
                        target = ft[p // kp // ry, p // kp % ry, p % kp]
                        for m in range(n_mid):
                            part = jnp.where(target == m, piece, 0.0)
                            sums[m] = part if p == 0 else sums[m] + part
                    return jnp.concatenate(sums, axis=0).astype(BF16)

                @pl.loop(1, n_grid)
                def _(s):
                    to = lax.rem(g + s, n_grid)
                    rs_send[h, to] = one_share(to)
                    copy_to(rs_send.at[h, to], rs_recv.at[h, g], rs_ssem.at[h, s], rs_rsem.at[h, g], r, to).start()

                rs_recv[h, g] = one_share(g)

    for h in range(PARTS):
        def take(s, total):
            src = lax.rem(g + n_grid - s, n_grid)
            copy_to(rs_send.at[h, src], rs_recv.at[h, src], rs_ssem.at[h, s], rs_rsem.at[h, src], r, src).wait_recv()
            return total + rs_recv[h, src].astype(F32)

        total = lax.fori_loop(1, n_grid, take, rs_recv[h, g].astype(F32))
        m_res[:, h * lpd:(h + 1) * lpd, :] = total.reshape(n_mid, lpd, bs)

    def send_mid(it):
        @pl.when(jnp.logical_not(top))
        def _():
            copy_to(m_halos[it].at[1], m_halos[it].at[n_mid + 1], mh_send.at[it, 0], mh_recv.at[it, 1], r - 1, g).start()

        @pl.when(jnp.logical_not(bottom))
        def _():
            copy_to(m_halos[it].at[n_mid], m_halos[it].at[0], mh_send.at[it, 1], mh_recv.at[it, 0], r + 1, g).start()

    def mid_block(it, up):
        block = m_halos[it].at[up * (n_mid + 1)]
        return copy_to(block, block, mh_send.at[it, up], mh_recv.at[it, up], r, g)

    start = m_res[...] * (1.0 / CENTRE)
    m_dir[...] = start
    m_halos[0][1:n_mid + 1] = start.astype(BF16)
    send_mid(0)
    weights[2].wait()
    weights[3].wait()

    nt = (((1,), (1,)), ((), ()))
    kp2 = mp.shape[1]
    for it in range(DEG):
        for up, on in ends:
            @pl.when(on)
            def _():
                mid_block(it, up).wait_recv()

        @pl.loop(0, n_mid)
        def _(i):
            total = None
            for k in range(mb.shape[1]):
                picked = m_halos[it][i + mc[i, k]]
                term = lax.dot_general(picked, mb[i, k], nt, preferred_element_type=F32)
                total = term if total is None else total + term
            left = m_res[i] - total
            m_res[i] = left
            if it < DEG - 1:
                alpha, beta = factors[it]
                old = m_dir[i]
                new = alpha * old + beta * left
                m_dir[i] = new
                m_halos[it + 1][i + 1] = new.astype(BF16)
                m_itr[i] = old + new if it == 0 else m_itr[i] + new

        if it < DEG - 1:
            send_mid(it + 1)
        if it == DEG - 2:
            ag_send[...] = m_itr[...].astype(BF16)
            ag_recv[g] = ag_send[...]

            @pl.loop(1, n_grid)
            def _(s):
                to = lax.rem(g + s, n_grid)
                copy_to(ag_send, ag_recv.at[g], ag_ssem.at[s], ag_rsem.at[g], r, to).start()

    sums = [None] * C3
    for i in range(n_mid):
        rounded = m_res[i].astype(BF16)
        for k in range(kp2):
            piece = jnp.dot(rounded, mp[i, k], preferred_element_type=F32)
            for m in range(C3):
                part = jnp.where(mt[i, k] == m, piece, 0.0)
                sums[m] = part if sums[m] is None else sums[m] + part
    low = jnp.stack(sums[:half_c])
    high = jnp.stack(sums[half_c:])
    mine = jnp.where(core == 0, low, high)
    c_pair_send[...] = jnp.where(core == 0, high, low).astype(BF16)
    swap = copy_to(c_pair_send, c_pair_recv, cp_ssem.at[0], cp_rsem.at[0], mate, g)
    swap.start()
    swap.wait()
    mine = mine + c_pair_recv[...].astype(F32)
    c_z_send[...] = mine.astype(BF16)

    @pl.loop(1, n_pair)
    def _(s):
        copy_to(c_z_send, c_z_recv.at[s], cz_ssem.at[s], cz_rsem.at[s], lax.rem(r + 2 * s, n_row), g).start()

    def take_z(s, total):
        copy_to(c_z_send, c_z_recv.at[s], cz_ssem.at[s], cz_rsem.at[s], r, g).wait_recv()
        return total + c_z_recv[s].astype(F32)

    mine = lax.fori_loop(1, n_pair, take_z, mine)
    c_g_send[...] = mine.astype(BF16)

    @pl.loop(1, n_grid)
    def _(s):
        to = lax.rem(g + s, n_grid)
        copy_to(c_g_send, c_g_recv.at[g], cg_ssem.at[s], cg_rsem.at[g], r, to).start()

    c_g_recv[g] = c_g_send[...]
    copy_to(c_g_recv.at[g], c_all.at[g], ca_ssem.at[g], ca_rsem.at[g], mate, g).start()

    @pl.loop(1, n_grid)
    def _(s):
        src = lax.rem(g + n_grid - s, n_grid)
        copy_to(c_g_send, c_g_recv.at[src], cg_ssem.at[s], cg_rsem.at[src], r, g).wait_recv()
        copy_to(c_g_recv.at[src], c_all.at[src], ca_ssem.at[src], ca_rsem.at[src], mate, g).start()

    @pl.loop(1, n_grid)
    def _(s):
        src = lax.rem(g + n_grid - s, n_grid)
        copy_to(ag_send, ag_recv.at[src], ag_ssem.at[s], ag_rsem.at[src], r, g).wait_recv()

    def spread(turn, src, block):
        wide = block.astype(F32)
        for h in range(PARTS):
            rows = pl.ds(pl.multiple_of(h * width + src * lpd, lpd), lpd)
            turn[rows, :] = wide[h * lpd:(h + 1) * lpd]

    @pl.loop(0, n_mid)
    def _(m):
        for src in range(n_grid):
            spread(m_turn, src, ag_recv[src, m])
        m_out[m] = m_turn[...].T

    pltpu.make_async_copy(m_out, out_m, out_sem.at[1]).start()

    @pl.loop(0, n_grid)
    def _(src):
        copy_to(c_g_recv.at[src], c_all.at[src], ca_ssem.at[src], ca_rsem.at[src], mate, g).wait_recv()

    for m in range(half_c):
        for other in range(2):
            source = c_all if other else c_g_recv
            for src in range(n_grid):
                spread(c_turn, src, source[src, m])
            place = m + half_c * (other + core - 2 * other * core)
            c_out[place] = c_turn[...].T

    pltpu.make_async_copy(c_out, out_c, out_sem.at[2]).start()

    for it in range(DEG):
        for h in range(PARTS):
            for y in range(ry):
                to = g + 2 * y - 1

                @pl.when(jnp.logical_and(to >= 0, to < n_grid))
                def _():
                    for x in range(rx):
                        grid_block(it, h, 1 - y, x).wait_send()

            for up, on in ends:
                @pl.when(on)
                def _():
                    for y in range(ry):
                        row_block(it, h, up, y).wait_send()
                    for side, there in sides:
                        @pl.when(there)
                        def _():
                            corner(it, h, up, side).wait_send()
        for up, on in ends:
            @pl.when(on)
            def _():
                mid_block(it, up).wait_send()

    @pl.loop(1, n_grid)
    def _(s):
        to = lax.rem(g + s, n_grid)
        for h in range(PARTS):
            copy_to(rs_send.at[h, to], rs_recv.at[h, g], rs_ssem.at[h, s], rs_rsem.at[h, g], r, to).wait_send()
        copy_to(ag_send, ag_recv.at[g], ag_ssem.at[s], ag_rsem.at[g], r, to).wait_send()
        copy_to(c_g_send, c_g_recv.at[g], cg_ssem.at[s], cg_rsem.at[g], r, to).wait_send()

    @pl.loop(1, n_pair)
    def _(s):
        copy_to(c_z_send, c_z_recv.at[s], cz_ssem.at[s], cz_rsem.at[s], lax.rem(r + 2 * s, n_row), g).wait_send()

    @pl.loop(0, n_grid)
    def _(src):
        copy_to(c_g_recv.at[src], c_all.at[src], ca_ssem.at[src], ca_rsem.at[src], mate, g).wait_send()

    pltpu.make_async_copy(itr, out_f, out_sem.at[0]).wait()
    pltpu.make_async_copy(m_out, out_m, out_sem.at[1]).wait()
    pltpu.make_async_copy(c_out, out_c, out_sem.at[2]).wait()


def body(n_row, n_grid, b, fb, fc, fp, ft, mb, mc, mp, mt):
    rx, ry, bs, loads = b.shape
    width = loads // PARTS
    lpd = width // n_grid
    LPD = lpd * PARTS
    n_mid = mb.shape[0]
    kp = fp.shape[2]
    half_c = C3 // 2
    any_spec = pl.BlockSpec(memory_space=pl.ANY)
    smem = pl.BlockSpec(memory_space=pltpu.SMEM)
    vmem = pltpu.VMEM
    dma = pltpu.SemaphoreType.DMA
    flops = 2 * bs * bs * loads * rx * ry * (fb.shape[2] * DEG + kp)
    return pl.pallas_call(
        functools.partial(kernel, n_row, n_grid),
        out_shape=(
            jax.ShapeDtypeStruct(b.shape, F32),
            jax.ShapeDtypeStruct((n_mid, bs, loads), F32),
            jax.ShapeDtypeStruct((C3, bs, loads), F32),
        ),
        in_specs=[any_spec, any_spec, smem, any_spec, smem, any_spec, smem, any_spec, smem],
        out_specs=(any_spec, any_spec, any_spec),
        scratch_shapes=[
            vmem(b.shape, F32),
            vmem(b.shape, F32),
            vmem(b.shape, F32),
            vmem(fb.shape, BF16),
            vmem(fp.shape, BF16),
            vmem(mb.shape, BF16),
            vmem(mp.shape, BF16),
            [[vmem((ry + 2, rx + 2, bs, width), BF16)] * PARTS] * DEG,
            vmem((rx * ry * kp, width, bs), F32),
            vmem((PARTS, n_grid, n_mid * lpd, bs), BF16),
            vmem((PARTS, n_grid, n_mid * lpd, bs), BF16),
            [vmem((n_mid + 2, LPD, bs), BF16)] * DEG,
            vmem((n_mid, LPD, bs), F32),
            vmem((n_mid, LPD, bs), F32),
            vmem((n_mid, LPD, bs), F32),
            vmem((n_mid, LPD, bs), BF16),
            vmem((n_grid, n_mid, LPD, bs), BF16),
            vmem((loads, bs), F32),
            vmem((n_mid, bs, loads), F32),
            vmem((half_c, LPD, bs), BF16),
            vmem((half_c, LPD, bs), BF16),
            vmem((half_c, LPD, bs), BF16),
            vmem((n_row // 2, half_c, LPD, bs), BF16),
            vmem((half_c, LPD, bs), BF16),
            vmem((n_grid, half_c, LPD, bs), BF16),
            vmem((n_grid, half_c, LPD, bs), BF16),
            vmem((loads, bs), F32),
            vmem((C3, bs, loads), F32),
            dma((rx,)), dma((3,)), dma((4,)),
            dma((DEG, PARTS, 2, rx)), dma((DEG, PARTS, 2, rx)),
            dma((DEG, PARTS, 2, ry)), dma((DEG, PARTS, 2, ry)),
            dma((DEG, PARTS, 2, 2)), dma((DEG, PARTS, 2, 2)),
            dma((PARTS, n_grid)), dma((PARTS, n_grid)),
            dma((DEG, 2)), dma((DEG, 2)),
            dma((n_grid,)), dma((n_grid,)),
            dma((1,)), dma((1,)),
            dma((n_row // 2,)), dma((n_row // 2,)),
            dma((n_grid,)), dma((n_grid,)),
            dma((n_grid,)), dma((n_grid,)),
        ],
        compiler_params=pltpu.CompilerParams(
            collective_id=0, has_side_effects=True, vmem_limit_bytes=56 * 1024 * 1024
        ),
        cost_estimate=pl.CostEstimate(flops=flops, bytes_accessed=13_000_000, transcendentals=0),
    )(b, fb, fc, fp, ft, mb, mc, mp, mt)


def solution(mesh):
    placed = (
        P("row", "grid", None, None),
        P("row", "grid", None, None, None),
        P("row", "grid", None),
        P("row", "grid", None, None, None),
        P("row", "grid", None),
        P("row", None, None, None),
        P("row", None),
        P("row", None, None, None),
        P("row", None),
    )
    return jax.shard_map(
        functools.partial(body, mesh.shape["row"], mesh.shape["grid"]),
        mesh=mesh,
        in_specs=placed,
        out_specs=(P("row", "grid", None, None), P("row", None, None), P()),
        check_vma=False,
    )
```

```python
import functools

import jax
import jax.numpy as jnp
from jax import lax
from jax.experimental import pallas as pl
from jax.experimental.pallas import tpu as pltpu
from jax.sharding import PartitionSpec as P

MESH = pl.DeviceIdType.MESH
F32 = jnp.float32
BF16 = jnp.bfloat16

C3 = 4
DEG = 3
PARTS = 2
GROUP = 4
REACH = DEG

cheb_low = 0.6
cheb_high = 6.0
CENTRE = 0.5 * (cheb_high + cheb_low)
HALF = 0.5 * (cheb_high - cheb_low)


def sweep_factors():
    ratio = CENTRE / HALF
    rho = 1.0 / ratio
    factors = []
    for _ in range(DEG - 1):
        rho_next = 1.0 / (2.0 * ratio - rho)
        factors.append((rho_next * rho, 2.0 * rho_next / HALF))
        rho = rho_next
    return factors


def copy_to(src, dst, send, recv, row, grid):
    return pltpu.make_async_remote_copy(
        src_ref=src, dst_ref=dst, send_sem=send, recv_sem=recv, device_id=(row, grid), device_id_type=MESH
    )


def kernel(
    n_row, n_grid,
    b_hbm, fb_hbm, fc, fp_hbm, ft, mb_hbm, mc, mp_hbm, mt,
    out_f, out_m, out_c,
    res, dirn, itr, fb, fp, mb, mp, halos, pieces, rs_send, rs_recv,
    m_halos, cols_send, cols_recv, edge_send, m_res, m_dir, m_itr, ag_send, ag_recv, m_turn, m_out,
    c_pair_send, c_pair_recv, c_z_send, c_z_recv, c_g_send, c_g_recv, c_all, c_turn, c_out,
    in_sem, out_sem, w_sem,
    g_send, g_recv, r_send, r_recv, k_send, k_recv,
    rs_ssem, rs_rsem, mh_send, mh_recv, mb_send, mb_recv, mc_send, mc_recv, ag_ssem, ag_rsem,
    cp_ssem, cp_rsem, cz_ssem, cz_rsem, cg_ssem, cg_rsem, ca_ssem, ca_rsem,
):
    r = lax.axis_index("row")
    g = lax.axis_index("grid")
    rx, ry = res.shape[0], res.shape[1]
    bs, loads = res.shape[2], res.shape[3]
    width = loads // PARTS
    lpd = width // n_grid
    LPD = lpd * PARTS
    n_mid = mb_hbm.shape[0]
    k2 = mb.shape[1]
    n_pair = n_row // 2
    core = lax.rem(r, 2)
    mate = r + 1 - 2 * core
    top, bottom = r == 0, r == n_row - 1
    first, last = g == 0, g == n_grid - 1
    half_c = C3 // 2

    for x in range(rx):
        pltpu.make_async_copy(b_hbm.at[x], res.at[x], in_sem.at[x]).start()
    weights = (
        pltpu.make_async_copy(fb_hbm, fb, w_sem.at[0]),
        pltpu.make_async_copy(fp_hbm, fp, w_sem.at[1]),
        pltpu.make_async_copy(mb_hbm, mb.at[pl.ds(REACH - 1, mb_hbm.shape[0])], w_sem.at[2]),
        pltpu.make_async_copy(mp_hbm, mp, w_sem.at[3]),
    )
    for w in weights:
        w.start()

    barrier = pltpu.get_barrier_semaphore()

    def greet(row, grid):
        pl.semaphore_signal(barrier, inc=1, device_id=(row, grid), device_id_type=MESH)

    @pl.loop(1, n_grid)
    def _(s):
        greet(r, lax.rem(g + s, n_grid))

    @pl.loop(1, n_pair)
    def _(s):
        greet(lax.rem(r + 2 * s, n_row), g)

    greet(mate, g)
    outer = r - 1 + 2 * core
    has_outer = jnp.logical_and(outer >= 0, outer < n_row)

    @pl.when(has_outer)
    def _():
        greet(outer, g)

    zero = jnp.zeros((bs, width), BF16)

    def clear_row(xi):
        for it in range(DEG):
            for h in range(PARTS):
                for yi in range(ry + 2):
                    halos[it][h][yi, xi] = zero

    def clear_column(yi):
        for it in range(DEG):
            for h in range(PARTS):
                for xi in range(rx + 2):
                    halos[it][h][yi, xi] = zero

    def clear_mid(side):
        for e in range(REACH):
            m_res[side * (n_mid + REACH) + e] = jnp.zeros((LPD, bs), F32)
        cols_recv[side] = jnp.zeros(cols_recv.shape[1:], BF16)
        for e in range(REACH - 1):
            for k in range(k2):
                mb[side * (n_mid + REACH - 1) + e, k] = jnp.zeros((bs, bs), BF16)

    @pl.when(top)
    def _():
        clear_row(0)
        clear_mid(0)

    @pl.when(bottom)
    def _():
        clear_row(rx + 1)
        clear_mid(1)

    @pl.when(first)
    def _():
        clear_column(0)

    @pl.when(last)
    def _():
        clear_column(ry + 1)

    def send_block(it, h, x, y):
        src = halos[it][h].at[y + 1, x + 1]
        to = g + 2 * y - 1

        @pl.when(jnp.logical_and(to >= 0, to < n_grid))
        def _():
            dst = halos[it][h].at[3 * (1 - y), x + 1]
            copy_to(src, dst, g_send.at[it, h, y, x], g_recv.at[it, h, 1 - y, x], r, to).start()

        @pl.when(jnp.logical_and(x == 0, jnp.logical_not(top)))
        def _():
            dst = halos[it][h].at[y + 1, rx + 1]
            copy_to(src, dst, r_send.at[it, h, 0, y], r_recv.at[it, h, 1, y], r - 1, g).start()

        @pl.when(jnp.logical_and(x == rx - 1, jnp.logical_not(bottom)))
        def _():
            dst = halos[it][h].at[y + 1, 0]
            copy_to(src, dst, r_send.at[it, h, 1, y], r_recv.at[it, h, 0, y], r + 1, g).start()

    def grid_block(it, h, side, x):
        block = halos[it][h].at[3 * side, x + 1]
        return copy_to(block, block, g_send.at[it, h, 1 - side, x], g_recv.at[it, h, side, x], r, g)

    def corner(it, h, up, side):
        src = halos[it][h].at[3 * side, 1 + up * (rx - 1)]
        dst = halos[it][h].at[3 * side, (rx + 1) * (1 - up)]
        return copy_to(src, dst, k_send.at[it, h, up, side], k_recv.at[it, h, 1 - up, side], r - 1 + 2 * up, g)

    def row_block(it, h, up, y):
        block = halos[it][h].at[y + 1, (rx + 1) * up]
        return copy_to(block, block, r_send.at[it, h, up, y], r_recv.at[it, h, up, y], r, g)

    def corner_in(it, h, up, side):
        block = halos[it][h].at[3 * side, (rx + 1) * up]
        return copy_to(block, block, k_send.at[it, h, up, side], k_recv.at[it, h, up, side], r, g)

    sides = ((0, jnp.logical_not(first)), (1, jnp.logical_not(last)))
    ends = ((0, jnp.logical_not(top)), (1, jnp.logical_not(bottom)))

    def forward_corners(it, h):
        for side, there in sides:
            @pl.when(there)
            def _():
                for up, on in ends:
                    grid_block(it, h, side, up * (rx - 1)).wait_recv()

                    @pl.when(on)
                    def _():
                        corner(it, h, up, side).start()

    def wait_halo(it, h):
        for side, there in sides:
            @pl.when(there)
            def _():
                for x in range(1, rx - 1):
                    grid_block(it, h, side, x).wait_recv()
        for up, on in ends:
            @pl.when(on)
            def _():
                for y in range(ry):
                    row_block(it, h, up, y).wait_recv()
                for side, there in sides:
                    @pl.when(there)
                    def _():
                        corner_in(it, h, up, side).wait_recv()

    def order(t):
        return (rx - t // ry) % rx, t % ry

    def mid_matrix(up, q):
        e, k = q // k2, q % k2
        src = mb.at[up * n_mid + (1 - up) * (REACH - 1) + e, k]
        dst = mb.at[(1 - up) * (n_mid + REACH - 1) + e, k]
        return copy_to(src, dst, mb_send.at[up, q], mb_recv.at[1 - up, q], r - 1 + 2 * up, g)

    def mid_columns(up):
        return copy_to(cols_send.at[up], cols_recv.at[1 - up], mc_send.at[up], mc_recv.at[1 - up], r - 1 + 2 * up, g)

    def mid_edge(up):
        src = edge_send.at[up]
        dst = m_res.at[pl.ds((1 - up) * (n_mid + REACH), REACH)]
        return copy_to(src, dst, mh_send.at[up], mh_recv.at[1 - up], r - 1 + 2 * up, g)

    for up in range(2):
        for e in range(REACH - 1):
            for k in range(k2):
                own = mc[k, up * (n_mid - REACH + 1) + e].astype(F32)
                cols_send[up, e, k] = jnp.full((LPD, bs), own, F32).astype(BF16)

    for x in range(rx):
        pltpu.make_async_copy(b_hbm.at[x], res.at[x], in_sem.at[x]).wait()
    for h in range(PARTS):
        cols = slice(h * width, (h + 1) * width)

        @pl.loop(0, rx * ry)
        def _(t):
            x, y = order(t)
            start = res[x, y, :, cols] * (1.0 / CENTRE)
            halos[0][h][y + 1, x + 1] = start.astype(BF16)
            if h == 0:
                @pl.when(t == 0)
                def _():
                    pl.semaphore_wait(barrier, n_grid - 1 + n_pair + jnp.where(has_outer, 1, 0))
            send_block(0, h, x, y)
            dirn[x, y, :, cols] = start

    weights[0].wait()
    weights[1].wait()
    factors = sweep_factors()
    n_pieces = pieces.shape[0]
    kp = fp.shape[2]

    for it in range(DEG):
        for h in range(PARTS):
            cols = slice(h * width, (h + 1) * width)
            if h == 0:
                forward_corners(it, h)
            wait_halo(it, h)
            phase = it * PARTS + h
            if phase == 0:
                weights[2].wait()
            for up, on in ends:
                @pl.when(on)
                def _():
                    if phase == 0:
                        mid_columns(up).start()
                    for q in range(phase, (REACH - 1) * k2, DEG * PARTS):
                        mid_matrix(up, q).start()

            def products(x, y):
                total = None
                for k in range(fb.shape[2]):
                    c = fc[x, y, k]
                    cx = lax.shift_right_logical(c * 11, 5)
                    picked = halos[it][h][y + c - 3 * cx, x + cx]
                    term = jnp.dot(fb[x, y, k], picked, preferred_element_type=F32)
                    total = term if total is None else total + term
                return total

            def update(x, y, total):
                left = res[x, y, :, cols] - total
                if it < DEG - 1:
                    res[x, y, :, cols] = left
                    alpha, beta = factors[it]
                    old = dirn[x, y, :, cols]
                    new = alpha * old + beta * left
                    halos[it + 1][h][y + 1, x + 1] = new.astype(BF16)
                    if it == 0:
                        dirn[x, y, :, cols] = new
                        itr[x, y, :, cols] = old + new
                    else:
                        itr[x, y, :, cols] = itr[x, y, :, cols] + new
                else:
                    turned = left.astype(BF16).T
                    for k in range(kp):
                        pieces[(x * ry + y) * kp + k] = jnp.dot(turned, fp[x, y, k], preferred_element_type=F32)

            def several(blocks):
                totals = [products(x, y) for x, y in blocks]
                for (x, y), total in zip(blocks, totals):
                    update(x, y, total)
                if it < DEG - 1:
                    for x, y in blocks:
                        send_block(it + 1, h, x, y)

            if GROUP == rx * ry:
                several([order(t) for t in range(rx * ry)])
            else:
                @pl.loop(0, rx * ry // GROUP)
                def _(t):
                    several([order(t * GROUP + u) for u in range(GROUP)])
                    if h + 1 < PARTS:
                        @pl.when(t == 0)
                        def _():
                            forward_corners(it, h + 1)

            if it == DEG - 2 and h == PARTS - 1:
                pltpu.make_async_copy(itr, out_f, out_sem.at[0]).start()

            if it == DEG - 1:
                def one_share(to):
                    rows = pl.ds(pl.multiple_of(to * lpd, lpd), lpd)
                    sums = [None] * n_mid
                    for p in range(n_pieces):
                        piece = pieces[p, rows, :]
                        target = ft[p // kp % ry, p % kp, p // kp // ry]
                        for m in range(n_mid):
                            part = jnp.where(target == m, piece, 0.0)
                            sums[m] = part if p == 0 else sums[m] + part
                    return jnp.concatenate(sums, axis=0).astype(BF16)

                @pl.loop(0, n_grid // 2)
                def _(q):
                    near = [(2 * q + u + 1, lax.rem(g + 2 * q + u + 1, n_grid)) for u in range(2)]
                    for (_, to), share in zip(near, [one_share(to) for _, to in near]):
                        rs_send[h, to] = share
                    for s, to in near:
                        @pl.when(s < n_grid)
                        def _():
                            copy_to(
                                rs_send.at[h, to], rs_recv.at[h, g], rs_ssem.at[h, s], rs_rsem.at[h, g], r, to
                            ).start()

    for h in range(PARTS):
        def take(s, total):
            src = lax.rem(g + n_grid - s, n_grid)
            copy_to(rs_send.at[h, src], rs_recv.at[h, src], rs_ssem.at[h, s], rs_rsem.at[h, src], r, src).wait_recv()
            return total + rs_recv[h, src].astype(F32)

        total = lax.fori_loop(1, n_grid, take, rs_send[h, g].astype(F32))
        m_res[REACH:REACH + n_mid, h * lpd:(h + 1) * lpd, :] = total.reshape(n_mid, lpd, bs)

    for up, on in ends:
        @pl.when(on)
        def _():
            edge_send[up] = m_res[up * n_mid + (1 - up) * REACH:up * n_mid + (1 - up) * REACH + REACH]
            mid_edge(up).start()
    weights[3].wait()
    for up, on in ends:
        @pl.when(on)
        def _():
            mid_columns(1 - up).wait_recv()
            for q in range((REACH - 1) * k2):
                mid_matrix(1 - up, q).wait_recv()
            mid_edge(1 - up).wait_recv()

    start = m_res[...] * (1.0 / CENTRE)
    m_dir[...] = start
    m_halos[0][...] = start.astype(BF16)

    nt = (((1,), (1,)), ((), ()))
    kp2 = mp.shape[1]
    for it in range(DEG):
        def mid_products(e):
            total = None
            for k in range(k2):
                if REACH <= e < REACH + n_mid:
                    picked = m_halos[it][e - 1 + mc[k, e - REACH]]
                else:
                    side = int(e >= REACH)
                    where = cols_recv[side, e - 1 - side * (n_mid + REACH - 1), k].astype(F32)
                    near = [m_halos[it][e + d].astype(F32) for d in (-1, 0, 1)]
                    picked = jnp.where(where == 0.0, near[0], jnp.where(where == 1.0, near[1], near[2])).astype(BF16)
                term = lax.dot_general(picked, mb[e - 1, k], nt, preferred_element_type=F32)
                total = term if total is None else total + term
            return total

        def mid_update(e, total):
            left = m_res[e] - total
            m_res[e] = left
            if it < DEG - 1:
                alpha, beta = factors[it]
                old = m_dir[e]
                new = alpha * old + beta * left
                m_dir[e] = new
                m_halos[it + 1][e] = new.astype(BF16)
                if REACH <= e < REACH + n_mid:
                    i = e - REACH
                    m_itr[i] = old + new if it == 0 else m_itr[i] + new

        rows = range(it + 1, n_mid + 2 * REACH - 1 - it)
        totals = [mid_products(e) for e in rows]
        for e, total in zip(rows, totals):
            mid_update(e, total)

        if it == DEG - 2:
            ag_send[...] = m_itr[...].astype(BF16)
            ag_recv[g] = ag_send[...]

            @pl.loop(1, n_grid)
            def _(s):
                to = lax.rem(g + s, n_grid)
                copy_to(ag_send, ag_recv.at[g], ag_ssem.at[s], ag_rsem.at[g], r, to).start()

    sums = [None] * C3
    for i in range(n_mid):
        rounded = m_res[REACH + i].astype(BF16)
        for k in range(kp2):
            piece = jnp.dot(rounded, mp[i, k], preferred_element_type=F32)
            for m in range(C3):
                part = jnp.where(mt[k, i] == m, piece, 0.0)
                sums[m] = part if sums[m] is None else sums[m] + part
    low = jnp.stack(sums[:half_c])
    high = jnp.stack(sums[half_c:])
    mine = jnp.where(core == 0, low, high)
    c_pair_send[...] = jnp.where(core == 0, high, low).astype(BF16)
    swap = copy_to(c_pair_send, c_pair_recv, cp_ssem.at[0], cp_rsem.at[0], mate, g)
    swap.start()
    swap.wait()
    mine = mine + c_pair_recv[...].astype(F32)
    c_z_send[...] = mine.astype(BF16)

    @pl.loop(1, n_pair)
    def _(s):
        copy_to(c_z_send, c_z_recv.at[s], cz_ssem.at[s], cz_rsem.at[s], lax.rem(r + 2 * s, n_row), g).start()

    def take_z(s, total):
        copy_to(c_z_send, c_z_recv.at[s], cz_ssem.at[s], cz_rsem.at[s], r, g).wait_recv()
        return total + c_z_recv[s].astype(F32)

    mine = lax.fori_loop(1, n_pair, take_z, mine)
    c_g_send[...] = mine.astype(BF16)

    @pl.loop(1, n_grid)
    def _(s):
        to = lax.rem(g + s, n_grid)
        copy_to(c_g_send, c_g_recv.at[g], cg_ssem.at[s], cg_rsem.at[g], r, to).start()

    c_g_recv[g] = c_g_send[...]
    copy_to(c_g_recv.at[g], c_all.at[g], ca_ssem.at[g], ca_rsem.at[g], mate, g).start()

    @pl.loop(1, n_grid)
    def _(s):
        src = lax.rem(g + n_grid - s, n_grid)
        copy_to(ag_send, ag_recv.at[src], ag_ssem.at[s], ag_rsem.at[src], r, g).wait_recv()

    def spread(turn, src, block):
        wide = block.astype(F32)
        for h in range(PARTS):
            rows = pl.ds(pl.multiple_of(h * width + src * lpd, lpd), lpd)
            turn[rows, :] = wide[h * lpd:(h + 1) * lpd]

    @pl.loop(0, n_mid)
    def _(m):
        for src in range(n_grid):
            spread(m_turn, src, ag_recv[src, m])
        m_out[m] = m_turn[...].T

    pltpu.make_async_copy(m_out, out_m, out_sem.at[1]).start()

    @pl.loop(1, n_grid)
    def _(s):
        src = lax.rem(g + n_grid - s, n_grid)
        copy_to(c_g_send, c_g_recv.at[src], cg_ssem.at[s], cg_rsem.at[src], r, g).wait_recv()
        copy_to(c_g_recv.at[src], c_all.at[src], ca_ssem.at[src], ca_rsem.at[src], mate, g).start()

    @pl.loop(0, n_grid)
    def _(src):
        copy_to(c_g_recv.at[src], c_all.at[src], ca_ssem.at[src], ca_rsem.at[src], mate, g).wait_recv()

    for m in range(half_c):
        for other in range(2):
            source = c_all if other else c_g_recv
            for src in range(n_grid):
                spread(c_turn, src, source[src, m])
            place = m + half_c * (other + core - 2 * other * core)
            c_out[place] = c_turn[...].T

    pltpu.make_async_copy(c_out, out_c, out_sem.at[2]).start()

    for up, on in ends:
        @pl.when(on)
        def _():
            mid_columns(up).wait_send()
            mid_edge(up).wait_send()
            for q in range((REACH - 1) * k2):
                mid_matrix(up, q).wait_send()

    for it in range(DEG):
        for h in range(PARTS):
            for y in range(ry):
                to = g + 2 * y - 1

                @pl.when(jnp.logical_and(to >= 0, to < n_grid))
                def _():
                    for x in range(rx):
                        grid_block(it, h, 1 - y, x).wait_send()

            for up, on in ends:
                @pl.when(on)
                def _():
                    for y in range(ry):
                        row_block(it, h, up, y).wait_send()
                    for side, there in sides:
                        @pl.when(there)
                        def _():
                            corner(it, h, up, side).wait_send()

    @pl.loop(1, n_grid)
    def _(s):
        to = lax.rem(g + s, n_grid)
        for h in range(PARTS):
            copy_to(rs_send.at[h, to], rs_recv.at[h, g], rs_ssem.at[h, s], rs_rsem.at[h, g], r, to).wait_send()
        copy_to(ag_send, ag_recv.at[g], ag_ssem.at[s], ag_rsem.at[g], r, to).wait_send()
        copy_to(c_g_send, c_g_recv.at[g], cg_ssem.at[s], cg_rsem.at[g], r, to).wait_send()

    @pl.loop(1, n_pair)
    def _(s):
        copy_to(c_z_send, c_z_recv.at[s], cz_ssem.at[s], cz_rsem.at[s], lax.rem(r + 2 * s, n_row), g).wait_send()

    @pl.loop(0, n_grid)
    def _(src):
        copy_to(c_g_recv.at[src], c_all.at[src], ca_ssem.at[src], ca_rsem.at[src], mate, g).wait_send()

    pltpu.make_async_copy(itr, out_f, out_sem.at[0]).wait()
    pltpu.make_async_copy(m_out, out_m, out_sem.at[1]).wait()
    pltpu.make_async_copy(c_out, out_c, out_sem.at[2]).wait()


HAND = 4


def hand_over(f, m, c, out_f, out_m, out_c, hold_f, hold_m, hold_c, sem_in, sem_out):
    arriving, leaving = [], []
    for n, (src, hold, dst) in enumerate(((f, hold_f, out_f), (m, hold_m, out_m), (c, hold_c, out_c))):
        part = src.shape[0] // HAND
        for q in range(HAND):
            rows = pl.ds(q * part, part)
            arriving.append(pltpu.make_async_copy(src.at[rows], hold.at[rows], sem_in.at[n, q]))
            leaving.append(pltpu.make_async_copy(hold.at[rows], dst.at[rows], sem_out.at[n, q]))
    for copy in arriving:
        copy.start()
    for came, goes in zip(arriving, leaving):
        came.wait()
        goes.start()
    for copy in leaving:
        copy.wait()


def body(n_row, n_grid, b, fb, fc, fp, ft, mb, mc, mp, mt):
    rx, ry, bs, loads = b.shape
    width = loads // PARTS
    lpd = width // n_grid
    LPD = lpd * PARTS
    n_mid = mb.shape[0]
    kp = fp.shape[2]
    half_c = C3 // 2
    any_spec = pl.BlockSpec(memory_space=pl.ANY)
    smem = pl.BlockSpec(memory_space=pltpu.SMEM)
    vmem = pltpu.VMEM
    dma = pltpu.SemaphoreType.DMA
    flops = 2 * bs * bs * loads * rx * ry * (fb.shape[2] * DEG + kp)
    results = pl.pallas_call(
        functools.partial(kernel, n_row, n_grid),
        out_shape=(
            jax.ShapeDtypeStruct(b.shape, F32),
            jax.ShapeDtypeStruct((n_mid, bs, loads), F32),
            jax.ShapeDtypeStruct((C3, bs, loads), F32),
        ),
        in_specs=[any_spec, any_spec, smem, any_spec, smem, any_spec, smem, any_spec, smem],
        out_specs=(any_spec, any_spec, any_spec),
        scratch_shapes=[
            vmem(b.shape, F32),
            vmem(b.shape, F32),
            vmem(b.shape, F32),
            vmem(fb.shape, BF16),
            vmem(fp.shape, BF16),
            vmem((n_mid + 2 * REACH - 2,) + mb.shape[1:], BF16),
            vmem(mp.shape, BF16),
            [[vmem((ry + 2, rx + 2, bs, width), BF16)] * PARTS] * DEG,
            vmem((rx * ry * kp, width, bs), F32),
            vmem((PARTS, n_grid, n_mid * lpd, bs), BF16),
            vmem((PARTS, n_grid, n_mid * lpd, bs), BF16),
            [vmem((n_mid + 2 * REACH, LPD, bs), BF16)] * DEG,
            vmem((2, REACH - 1, mb.shape[1], LPD, bs), BF16),
            vmem((2, REACH - 1, mb.shape[1], LPD, bs), BF16),
            vmem((2, REACH, LPD, bs), F32),
            vmem((n_mid + 2 * REACH, LPD, bs), F32),
            vmem((n_mid + 2 * REACH, LPD, bs), F32),
            vmem((n_mid, LPD, bs), F32),
            vmem((n_mid, LPD, bs), BF16),
            vmem((n_grid, n_mid, LPD, bs), BF16),
            vmem((loads, bs), F32),
            vmem((n_mid, bs, loads), F32),
            vmem((half_c, LPD, bs), BF16),
            vmem((half_c, LPD, bs), BF16),
            vmem((half_c, LPD, bs), BF16),
            vmem((n_row // 2, half_c, LPD, bs), BF16),
            vmem((half_c, LPD, bs), BF16),
            vmem((n_grid, half_c, LPD, bs), BF16),
            vmem((n_grid, half_c, LPD, bs), BF16),
            vmem((loads, bs), F32),
            vmem((C3, bs, loads), F32),
            dma((rx,)), dma((3,)), dma((4,)),
            dma((DEG, PARTS, 2, rx)), dma((DEG, PARTS, 2, rx)),
            dma((DEG, PARTS, 2, ry)), dma((DEG, PARTS, 2, ry)),
            dma((DEG, PARTS, 2, 2)), dma((DEG, PARTS, 2, 2)),
            dma((PARTS, n_grid)), dma((PARTS, n_grid)),
            dma((2,)), dma((2,)),
            dma((2, (REACH - 1) * mb.shape[1])), dma((2, (REACH - 1) * mb.shape[1])),
            dma((2,)), dma((2,)),
            dma((n_grid,)), dma((n_grid,)),
            dma((1,)), dma((1,)),
            dma((n_row // 2,)), dma((n_row // 2,)),
            dma((n_grid,)), dma((n_grid,)),
            dma((n_grid,)), dma((n_grid,)),
        ],
        compiler_params=pltpu.CompilerParams(
            collective_id=0, has_side_effects=True, vmem_limit_bytes=56 * 1024 * 1024
        ),
        cost_estimate=pl.CostEstimate(flops=flops, bytes_accessed=13_000_000, transcendentals=0),
    )(b, fb, fc, fp, ft.transpose(1, 2, 0), mb, mc.T, mp, mt.T)
    return pl.pallas_call(
        hand_over,
        out_shape=tuple(jax.ShapeDtypeStruct(o.shape, o.dtype) for o in results),
        in_specs=[any_spec] * 3,
        out_specs=(any_spec,) * 3,
        scratch_shapes=[vmem(o.shape, o.dtype) for o in results] + [dma((3, HAND)), dma((3, HAND))],
        compiler_params=pltpu.CompilerParams(vmem_limit_bytes=56 * 1024 * 1024),
    )(*results)


def solution(mesh):
    placed = (
        P("row", "grid", None, None),
        P("row", "grid", None, None, None),
        P("row", "grid", None),
        P("row", "grid", None, None, None),
        P("row", "grid", None),
        P("row", None, None, None),
        P("row", None),
        P("row", None, None, None),
        P("row", None),
    )
    return jax.shard_map(
        functools.partial(body, mesh.shape["row"], mesh.shape["grid"]),
        mesh=mesh,
        in_specs=placed,
        out_specs=(P("row", "grid", None, None), P("row", None, None), P()),
        check_vma=False,
    )
```

```python
import functools

import jax
import jax.numpy as jnp
from jax import lax
from jax.experimental import pallas as pl
from jax.experimental.pallas import tpu as pltpu
from jax.sharding import PartitionSpec as P

MESH = pl.DeviceIdType.MESH
F32 = jnp.float32
BF16 = jnp.bfloat16

C3 = 4
DEG = 3
PARTS = 2
GROUP = 4
REACH = DEG

cheb_low = 0.6
cheb_high = 6.0
CENTRE = 0.5 * (cheb_high + cheb_low)
HALF = 0.5 * (cheb_high - cheb_low)


def sweep_factors():
    ratio = CENTRE / HALF
    rho = 1.0 / ratio
    factors = []
    for _ in range(DEG - 1):
        rho_next = 1.0 / (2.0 * ratio - rho)
        factors.append((rho_next * rho, 2.0 * rho_next / HALF))
        rho = rho_next
    return factors


def copy_to(src, dst, send, recv, row, grid):
    return pltpu.make_async_remote_copy(
        src_ref=src, dst_ref=dst, send_sem=send, recv_sem=recv, device_id=(row, grid), device_id_type=MESH
    )


def kernel(
    n_row, n_grid,
    b_hbm, fb_hbm, fc, fp_hbm, ft, mb_hbm, mc, mp_hbm, mt,
    out_f, out_m, out_c,
    res, dirn, itr, fb, fp, mb, mp, halos, pieces, rs_send, rs_recv,
    m_halos, cols_send, cols_recv, edge_send, m_res, m_dir, m_itr, ag_send, ag_recv, m_turn, m_out,
    c_pair_send, c_pair_recv, c_z_send, c_z_recv, c_g_send, c_g_recv, c_all, c_turn, c_out,
    in_sem, out_sem, w_sem,
    g_send, g_recv, r_send, r_recv, k_send, k_recv,
    rs_ssem, rs_rsem, mh_send, mh_recv, mb_send, mb_recv, mc_send, mc_recv, ag_ssem, ag_rsem,
    cp_ssem, cp_rsem, cz_ssem, cz_rsem, cg_ssem, cg_rsem, ca_ssem, ca_rsem,
):
    r = lax.axis_index("row")
    g = lax.axis_index("grid")
    rx, ry = res.shape[0], res.shape[1]
    bs, loads = res.shape[2], res.shape[3]
    width = loads // PARTS
    lpd = width // n_grid
    LPD = lpd * PARTS
    n_mid = mb_hbm.shape[0]
    k2 = mb.shape[1]
    n_pair = n_row // 2
    core = lax.rem(r, 2)
    mate = r + 1 - 2 * core
    top, bottom = r == 0, r == n_row - 1
    first, last = g == 0, g == n_grid - 1
    half_c = C3 // 2

    for x in range(rx):
        pltpu.make_async_copy(b_hbm.at[x], res.at[x], in_sem.at[x]).start()
    weights = (
        pltpu.make_async_copy(fb_hbm, fb, w_sem.at[0]),
        pltpu.make_async_copy(fp_hbm, fp, w_sem.at[1]),
        pltpu.make_async_copy(mb_hbm, mb.at[pl.ds(REACH - 1, mb_hbm.shape[0])], w_sem.at[2]),
        pltpu.make_async_copy(mp_hbm, mp, w_sem.at[3]),
    )
    for w in weights:
        w.start()

    barrier = pltpu.get_barrier_semaphore()

    def greet(row, grid):
        pl.semaphore_signal(barrier, inc=1, device_id=(row, grid), device_id_type=MESH)

    @pl.loop(1, n_grid)
    def _(s):
        greet(r, lax.rem(g + s, n_grid))

    @pl.loop(1, n_pair)
    def _(s):
        greet(lax.rem(r + 2 * s, n_row), g)

    greet(mate, g)
    outer = r - 1 + 2 * core
    has_outer = jnp.logical_and(outer >= 0, outer < n_row)

    @pl.when(has_outer)
    def _():
        greet(outer, g)

    zero = jnp.zeros((bs, width), BF16)

    def clear_row(xi):
        for it in range(DEG):
            for h in range(PARTS):
                for yi in range(ry + 2):
                    halos[it][h][yi, xi] = zero

    def clear_column(yi):
        for it in range(DEG):
            for h in range(PARTS):
                for xi in range(rx + 2):
                    halos[it][h][yi, xi] = zero

    def clear_mid(side):
        for e in range(REACH):
            m_res[side * (n_mid + REACH) + e] = jnp.zeros((LPD, bs), F32)
        cols_recv[side] = jnp.zeros(cols_recv.shape[1:], BF16)
        for e in range(REACH - 1):
            for k in range(k2):
                mb[side * (n_mid + REACH - 1) + e, k] = jnp.zeros((bs, bs), BF16)

    @pl.when(top)
    def _():
        clear_row(0)
        clear_mid(0)

    @pl.when(bottom)
    def _():
        clear_row(rx + 1)
        clear_mid(1)

    @pl.when(first)
    def _():
        clear_column(0)

    @pl.when(last)
    def _():
        clear_column(ry + 1)

    def send_block(it, h, x, y):
        src = halos[it][h].at[y + 1, x + 1]
        to = g + 2 * y - 1

        @pl.when(jnp.logical_and(to >= 0, to < n_grid))
        def _():
            dst = halos[it][h].at[3 * (1 - y), x + 1]
            copy_to(src, dst, g_send.at[it, h, y, x], g_recv.at[it, h, 1 - y, x], r, to).start()

        @pl.when(jnp.logical_and(x == 0, jnp.logical_not(top)))
        def _():
            dst = halos[it][h].at[y + 1, rx + 1]
            copy_to(src, dst, r_send.at[it, h, 0, y], r_recv.at[it, h, 1, y], r - 1, g).start()

        @pl.when(jnp.logical_and(x == rx - 1, jnp.logical_not(bottom)))
        def _():
            dst = halos[it][h].at[y + 1, 0]
            copy_to(src, dst, r_send.at[it, h, 1, y], r_recv.at[it, h, 0, y], r + 1, g).start()

    def grid_block(it, h, side, x):
        block = halos[it][h].at[3 * side, x + 1]
        return copy_to(block, block, g_send.at[it, h, 1 - side, x], g_recv.at[it, h, side, x], r, g)

    def corner(it, h, up, side):
        src = halos[it][h].at[3 * side, 1 + up * (rx - 1)]
        dst = halos[it][h].at[3 * side, (rx + 1) * (1 - up)]
        return copy_to(src, dst, k_send.at[it, h, up, side], k_recv.at[it, h, 1 - up, side], r - 1 + 2 * up, g)

    def row_block(it, h, up, y):
        block = halos[it][h].at[y + 1, (rx + 1) * up]
        return copy_to(block, block, r_send.at[it, h, up, y], r_recv.at[it, h, up, y], r, g)

    def corner_in(it, h, up, side):
        block = halos[it][h].at[3 * side, (rx + 1) * up]
        return copy_to(block, block, k_send.at[it, h, up, side], k_recv.at[it, h, up, side], r, g)

    sides = ((0, jnp.logical_not(first)), (1, jnp.logical_not(last)))
    ends = ((0, jnp.logical_not(top)), (1, jnp.logical_not(bottom)))

    def forward_corners(it, h):
        for side, there in sides:
            @pl.when(there)
            def _():
                for up, on in ends:
                    grid_block(it, h, side, up * (rx - 1)).wait_recv()

                    @pl.when(on)
                    def _():
                        corner(it, h, up, side).start()

    def wait_halo(it, h):
        for side, there in sides:
            @pl.when(there)
            def _():
                for x in range(1, rx - 1):
                    grid_block(it, h, side, x).wait_recv()
        for up, on in ends:
            @pl.when(on)
            def _():
                for y in range(ry):
                    row_block(it, h, up, y).wait_recv()
                for side, there in sides:
                    @pl.when(there)
                    def _():
                        corner_in(it, h, up, side).wait_recv()

    def order(t):
        return (rx - t // ry) % rx, t % ry

    def mid_matrix(up, q):
        e, k = q // k2, q % k2
        src = mb.at[up * n_mid + (1 - up) * (REACH - 1) + e, k]
        dst = mb.at[(1 - up) * (n_mid + REACH - 1) + e, k]
        return copy_to(src, dst, mb_send.at[up, q], mb_recv.at[1 - up, q], r - 1 + 2 * up, g)

    def mid_columns(up):
        return copy_to(cols_send.at[up], cols_recv.at[1 - up], mc_send.at[up], mc_recv.at[1 - up], r - 1 + 2 * up, g)

    def mid_edge(up):
        src = edge_send.at[up]
        dst = m_res.at[pl.ds((1 - up) * (n_mid + REACH), REACH)]
        return copy_to(src, dst, mh_send.at[up], mh_recv.at[1 - up], r - 1 + 2 * up, g)

    for up in range(2):
        for e in range(REACH - 1):
            for k in range(k2):
                own = mc[k, up * (n_mid - REACH + 1) + e].astype(F32)
                cols_send[up, e, k] = jnp.full((LPD, bs), own, F32).astype(BF16)

    for x in range(rx):
        pltpu.make_async_copy(b_hbm.at[x], res.at[x], in_sem.at[x]).wait()
    for h in range(PARTS):
        cols = slice(h * width, (h + 1) * width)

        @pl.loop(0, rx * ry)
        def _(t):
            x, y = order(t)
            start = res[x, y, :, cols] * (1.0 / CENTRE)
            halos[0][h][y + 1, x + 1] = start.astype(BF16)
            if h == 0:
                @pl.when(t == 0)
                def _():
                    pl.semaphore_wait(barrier, n_grid - 1 + n_pair + jnp.where(has_outer, 1, 0))
            send_block(0, h, x, y)
            dirn[x, y, :, cols] = start

    weights[0].wait()
    weights[1].wait()
    factors = sweep_factors()
    n_pieces = pieces.shape[0]
    kp = fp.shape[2]

    for it in range(DEG):
        for h in range(PARTS):
            cols = slice(h * width, (h + 1) * width)
            if h == 0:
                forward_corners(it, h)
            wait_halo(it, h)
            phase = it * PARTS + h
            if phase == 0:
                weights[2].wait()
            for up, on in ends:
                @pl.when(on)
                def _():
                    if phase == 0:
                        mid_columns(up).start()
                    for q in range(phase, (REACH - 1) * k2, DEG * PARTS):
                        mid_matrix(up, q).start()

            def products(x, y):
                total = None
                for k in range(fb.shape[2]):
                    c = fc[x, y, k]
                    cx = lax.shift_right_logical(c * 11, 5)
                    picked = halos[it][h][y + c - 3 * cx, x + cx]
                    term = jnp.dot(fb[x, y, k], picked, preferred_element_type=F32)
                    total = term if total is None else total + term
                return total

            def update(x, y, total):
                left = res[x, y, :, cols] - total
                if it < DEG - 1:
                    res[x, y, :, cols] = left
                    alpha, beta = factors[it]
                    old = dirn[x, y, :, cols]
                    new = alpha * old + beta * left
                    halos[it + 1][h][y + 1, x + 1] = new.astype(BF16)
                    if it == 0:
                        dirn[x, y, :, cols] = new
                        itr[x, y, :, cols] = old + new
                    else:
                        itr[x, y, :, cols] = itr[x, y, :, cols] + new
                else:
                    turned = left.astype(BF16).T
                    for k in range(kp):
                        pieces[(x * ry + y) * kp + k] = jnp.dot(turned, fp[x, y, k], preferred_element_type=F32)

            def several(blocks):
                totals = [products(x, y) for x, y in blocks]
                for (x, y), total in zip(blocks, totals):
                    update(x, y, total)
                if it < DEG - 1:
                    for x, y in blocks:
                        send_block(it + 1, h, x, y)

            if GROUP == rx * ry:
                several([order(t) for t in range(rx * ry)])
            else:
                @pl.loop(0, rx * ry // GROUP)
                def _(t):
                    several([order(t * GROUP + u) for u in range(GROUP)])
                    if h + 1 < PARTS:
                        @pl.when(t == 0)
                        def _():
                            forward_corners(it, h + 1)

            if it == DEG - 2 and h == PARTS - 1:
                pltpu.make_async_copy(itr, out_f, out_sem.at[0]).start()

            if it == DEG - 1:
                def one_share(to):
                    rows = pl.ds(pl.multiple_of(to * lpd, lpd), lpd)
                    sums = [None] * n_mid
                    for p in range(n_pieces):
                        piece = pieces[p, rows, :]
                        target = ft[p // kp % ry, p % kp, p // kp // ry]
                        for m in range(n_mid):
                            part = jnp.where(target == m, piece, 0.0)
                            sums[m] = part if p == 0 else sums[m] + part
                    pairs = [jnp.concatenate(sums[m:m + 2], axis=1) for m in range(0, n_mid, 2)]
                    return jnp.concatenate(pairs, axis=0).astype(BF16)

                @pl.loop(0, n_grid // 2)
                def _(q):
                    near = [(2 * q + u + 1, lax.rem(g + 2 * q + u + 1, n_grid)) for u in range(2)]
                    for (_, to), share in zip(near, [one_share(to) for _, to in near]):
                        rs_send[h, to] = share
                    for s, to in near:
                        @pl.when(s < n_grid)
                        def _():
                            copy_to(
                                rs_send.at[h, to], rs_recv.at[h, g], rs_ssem.at[h, s], rs_rsem.at[h, g], r, to
                            ).start()

    for h in range(PARTS):
        def take(s, total):
            src = lax.rem(g + n_grid - s, n_grid)
            copy_to(rs_send.at[h, src], rs_recv.at[h, src], rs_ssem.at[h, s], rs_rsem.at[h, src], r, src).wait_recv()
            return total + rs_recv[h, src].astype(F32)

        total = lax.fori_loop(1, n_grid, take, rs_send[h, g].astype(F32))
        for m in range(n_mid):
            half = total[m // 2 * lpd:(m // 2 + 1) * lpd, m % 2 * bs:(m % 2 + 1) * bs]
            m_res[REACH + m, h * lpd:(h + 1) * lpd, :] = half

    for up, on in ends:
        @pl.when(on)
        def _():
            edge_send[up] = m_res[up * n_mid + (1 - up) * REACH:up * n_mid + (1 - up) * REACH + REACH]
            mid_edge(up).start()
    weights[3].wait()
    for up, on in ends:
        @pl.when(on)
        def _():
            mid_columns(1 - up).wait_recv()
            for q in range((REACH - 1) * k2):
                mid_matrix(1 - up, q).wait_recv()
            mid_edge(1 - up).wait_recv()

    start = m_res[...] * (1.0 / CENTRE)
    m_dir[...] = start
    m_halos[0][...] = start.astype(BF16)

    nt = (((1,), (1,)), ((), ()))
    kp2 = mp.shape[1]
    for it in range(DEG):
        def mid_products(e):
            total = None
            for k in range(k2):
                if REACH <= e < REACH + n_mid:
                    picked = m_halos[it][e - 1 + mc[k, e - REACH]]
                else:
                    side = int(e >= REACH)
                    where = cols_recv[side, e - 1 - side * (n_mid + REACH - 1), k].astype(F32)
                    near = [m_halos[it][e + d].astype(F32) for d in (-1, 0, 1)]
                    picked = jnp.where(where == 0.0, near[0], jnp.where(where == 1.0, near[1], near[2])).astype(BF16)
                term = lax.dot_general(picked, mb[e - 1, k], nt, preferred_element_type=F32)
                total = term if total is None else total + term
            return total

        def mid_update(e, total):
            left = m_res[e] - total
            m_res[e] = left
            if it < DEG - 1:
                alpha, beta = factors[it]
                old = m_dir[e]
                new = alpha * old + beta * left
                m_dir[e] = new
                m_halos[it + 1][e] = new.astype(BF16)
                if REACH <= e < REACH + n_mid:
                    i = e - REACH
                    m_itr[i] = old + new if it == 0 else m_itr[i] + new

        rows = range(it + 1, n_mid + 2 * REACH - 1 - it)
        totals = [mid_products(e) for e in rows]
        for e, total in zip(rows, totals):
            mid_update(e, total)

        if it == DEG - 2:
            for q in range(n_mid // 2):
                ag_send[q] = jnp.concatenate([m_itr[2 * q], m_itr[2 * q + 1]], axis=1).astype(BF16)
            ag_recv[g] = ag_send[...]

            @pl.loop(1, n_grid)
            def _(s):
                to = lax.rem(g + s, n_grid)
                copy_to(ag_send, ag_recv.at[g], ag_ssem.at[s], ag_rsem.at[g], r, to).start()

    sums = [None] * C3
    for i in range(n_mid):
        rounded = m_res[REACH + i].astype(BF16)
        for k in range(kp2):
            piece = jnp.dot(rounded, mp[i, k], preferred_element_type=F32)
            for m in range(C3):
                part = jnp.where(mt[k, i] == m, piece, 0.0)
                sums[m] = part if sums[m] is None else sums[m] + part
    low = jnp.stack(sums[:half_c])
    high = jnp.stack(sums[half_c:])
    mine = jnp.where(core == 0, low, high)
    c_pair_send[...] = jnp.where(core == 0, high, low).astype(BF16)
    swap = copy_to(c_pair_send, c_pair_recv, cp_ssem.at[0], cp_rsem.at[0], mate, g)
    swap.start()
    swap.wait()
    mine = mine + c_pair_recv[...].astype(F32)
    c_z_send[...] = mine.astype(BF16)

    @pl.loop(1, n_pair)
    def _(s):
        copy_to(c_z_send, c_z_recv.at[s], cz_ssem.at[s], cz_rsem.at[s], lax.rem(r + 2 * s, n_row), g).start()

    def take_z(s, total):
        copy_to(c_z_send, c_z_recv.at[s], cz_ssem.at[s], cz_rsem.at[s], r, g).wait_recv()
        return total + c_z_recv[s].astype(F32)

    mine = lax.fori_loop(1, n_pair, take_z, mine)
    c_g_send[...] = mine.astype(BF16)

    @pl.loop(1, n_grid)
    def _(s):
        to = lax.rem(g + s, n_grid)
        copy_to(c_g_send, c_g_recv.at[g], cg_ssem.at[s], cg_rsem.at[g], r, to).start()

    c_g_recv[g] = c_g_send[...]
    copy_to(c_g_recv.at[g], c_all.at[g], ca_ssem.at[g], ca_rsem.at[g], mate, g).start()

    @pl.loop(1, n_grid)
    def _(s):
        src = lax.rem(g + n_grid - s, n_grid)
        copy_to(ag_send, ag_recv.at[src], ag_ssem.at[s], ag_rsem.at[src], r, g).wait_recv()

    def spread(turn, src, block):
        wide = block.astype(F32)
        for h in range(PARTS):
            rows = pl.ds(pl.multiple_of(h * width + src * lpd, lpd), lpd)
            turn[rows, :] = wide[h * lpd:(h + 1) * lpd]

    @pl.loop(0, n_mid // 2)
    def _(q):
        for src in range(n_grid):
            spread(m_turn, src, ag_recv[src, q])
        turned = m_turn[...].T
        m_out[2 * q] = turned[:bs]
        m_out[2 * q + 1] = turned[bs:]

    pltpu.make_async_copy(m_out, out_m, out_sem.at[1]).start()

    @pl.loop(1, n_grid)
    def _(s):
        src = lax.rem(g + n_grid - s, n_grid)
        copy_to(c_g_send, c_g_recv.at[src], cg_ssem.at[s], cg_rsem.at[src], r, g).wait_recv()
        copy_to(c_g_recv.at[src], c_all.at[src], ca_ssem.at[src], ca_rsem.at[src], mate, g).start()

    @pl.loop(0, n_grid)
    def _(src):
        copy_to(c_g_recv.at[src], c_all.at[src], ca_ssem.at[src], ca_rsem.at[src], mate, g).wait_recv()

    for m in range(half_c):
        for other in range(2):
            source = c_all if other else c_g_recv
            for src in range(n_grid):
                spread(c_turn, src, source[src, m])
            place = m + half_c * (other + core - 2 * other * core)
            c_out[place] = c_turn[...].T

    pltpu.make_async_copy(c_out, out_c, out_sem.at[2]).start()

    for up, on in ends:
        @pl.when(on)
        def _():
            mid_columns(up).wait_send()
            mid_edge(up).wait_send()
            for q in range((REACH - 1) * k2):
                mid_matrix(up, q).wait_send()

    for it in range(DEG):
        for h in range(PARTS):
            for y in range(ry):
                to = g + 2 * y - 1

                @pl.when(jnp.logical_and(to >= 0, to < n_grid))
                def _():
                    for x in range(rx):
                        grid_block(it, h, 1 - y, x).wait_send()

            for up, on in ends:
                @pl.when(on)
                def _():
                    for y in range(ry):
                        row_block(it, h, up, y).wait_send()
                    for side, there in sides:
                        @pl.when(there)
                        def _():
                            corner(it, h, up, side).wait_send()

    @pl.loop(1, n_grid)
    def _(s):
        to = lax.rem(g + s, n_grid)
        for h in range(PARTS):
            copy_to(rs_send.at[h, to], rs_recv.at[h, g], rs_ssem.at[h, s], rs_rsem.at[h, g], r, to).wait_send()
        copy_to(ag_send, ag_recv.at[g], ag_ssem.at[s], ag_rsem.at[g], r, to).wait_send()
        copy_to(c_g_send, c_g_recv.at[g], cg_ssem.at[s], cg_rsem.at[g], r, to).wait_send()

    @pl.loop(1, n_pair)
    def _(s):
        copy_to(c_z_send, c_z_recv.at[s], cz_ssem.at[s], cz_rsem.at[s], lax.rem(r + 2 * s, n_row), g).wait_send()

    @pl.loop(0, n_grid)
    def _(src):
        copy_to(c_g_recv.at[src], c_all.at[src], ca_ssem.at[src], ca_rsem.at[src], mate, g).wait_send()

    pltpu.make_async_copy(itr, out_f, out_sem.at[0]).wait()
    pltpu.make_async_copy(m_out, out_m, out_sem.at[1]).wait()
    pltpu.make_async_copy(c_out, out_c, out_sem.at[2]).wait()


HAND = 4


def hand_over(f, m, c, out_f, out_m, out_c, hold_f, hold_m, hold_c, sem_in, sem_out):
    arriving, leaving = [], []
    for n, (src, hold, dst) in enumerate(((f, hold_f, out_f), (m, hold_m, out_m), (c, hold_c, out_c))):
        part = src.shape[0] // HAND
        for q in range(HAND):
            rows = pl.ds(q * part, part)
            arriving.append(pltpu.make_async_copy(src.at[rows], hold.at[rows], sem_in.at[n, q]))
            leaving.append(pltpu.make_async_copy(hold.at[rows], dst.at[rows], sem_out.at[n, q]))
    for copy in arriving:
        copy.start()
    for came, goes in zip(arriving, leaving):
        came.wait()
        goes.start()
    for copy in leaving:
        copy.wait()


def body(n_row, n_grid, b, fb, fc, fp, ft, mb, mc, mp, mt):
    rx, ry, bs, loads = b.shape
    width = loads // PARTS
    lpd = width // n_grid
    LPD = lpd * PARTS
    n_mid = mb.shape[0]
    kp = fp.shape[2]
    half_c = C3 // 2
    any_spec = pl.BlockSpec(memory_space=pl.ANY)
    smem = pl.BlockSpec(memory_space=pltpu.SMEM)
    vmem = pltpu.VMEM
    dma = pltpu.SemaphoreType.DMA
    flops = 2 * bs * bs * loads * rx * ry * (fb.shape[2] * DEG + kp)
    results = pl.pallas_call(
        functools.partial(kernel, n_row, n_grid),
        out_shape=(
            jax.ShapeDtypeStruct(b.shape, F32),
            jax.ShapeDtypeStruct((n_mid, bs, loads), F32),
            jax.ShapeDtypeStruct((C3, bs, loads), F32),
        ),
        in_specs=[any_spec, any_spec, smem, any_spec, smem, any_spec, smem, any_spec, smem],
        out_specs=(any_spec, any_spec, any_spec),
        scratch_shapes=[
            vmem(b.shape, F32),
            vmem(b.shape, F32),
            vmem(b.shape, F32),
            vmem(fb.shape, BF16),
            vmem(fp.shape, BF16),
            vmem((n_mid + 2 * REACH - 2,) + mb.shape[1:], BF16),
            vmem(mp.shape, BF16),
            [[vmem((ry + 2, rx + 2, bs, width), BF16)] * PARTS] * DEG,
            vmem((rx * ry * kp, width, bs), F32),
            vmem((PARTS, n_grid, n_mid // 2 * lpd, 2 * bs), BF16),
            vmem((PARTS, n_grid, n_mid // 2 * lpd, 2 * bs), BF16),
            [vmem((n_mid + 2 * REACH, LPD, bs), BF16)] * DEG,
            vmem((2, REACH - 1, mb.shape[1], LPD, bs), BF16),
            vmem((2, REACH - 1, mb.shape[1], LPD, bs), BF16),
            vmem((2, REACH, LPD, bs), F32),
            vmem((n_mid + 2 * REACH, LPD, bs), F32),
            vmem((n_mid + 2 * REACH, LPD, bs), F32),
            vmem((n_mid, LPD, bs), F32),
            vmem((n_mid // 2, LPD, 2 * bs), BF16),
            vmem((n_grid, n_mid // 2, LPD, 2 * bs), BF16),
            vmem((loads, 2 * bs), F32),
            vmem((n_mid, bs, loads), F32),
            vmem((half_c, LPD, bs), BF16),
            vmem((half_c, LPD, bs), BF16),
            vmem((half_c, LPD, bs), BF16),
            vmem((n_row // 2, half_c, LPD, bs), BF16),
            vmem((half_c, LPD, bs), BF16),
            vmem((n_grid, half_c, LPD, bs), BF16),
            vmem((n_grid, half_c, LPD, bs), BF16),
            vmem((loads, bs), F32),
            vmem((C3, bs, loads), F32),
            dma((rx,)), dma((3,)), dma((4,)),
            dma((DEG, PARTS, 2, rx)), dma((DEG, PARTS, 2, rx)),
            dma((DEG, PARTS, 2, ry)), dma((DEG, PARTS, 2, ry)),
            dma((DEG, PARTS, 2, 2)), dma((DEG, PARTS, 2, 2)),
            dma((PARTS, n_grid)), dma((PARTS, n_grid)),
            dma((2,)), dma((2,)),
            dma((2, (REACH - 1) * mb.shape[1])), dma((2, (REACH - 1) * mb.shape[1])),
            dma((2,)), dma((2,)),
            dma((n_grid,)), dma((n_grid,)),
            dma((1,)), dma((1,)),
            dma((n_row // 2,)), dma((n_row // 2,)),
            dma((n_grid,)), dma((n_grid,)),
            dma((n_grid,)), dma((n_grid,)),
        ],
        compiler_params=pltpu.CompilerParams(
            collective_id=0, has_side_effects=True, vmem_limit_bytes=56 * 1024 * 1024
        ),
        cost_estimate=pl.CostEstimate(flops=flops, bytes_accessed=13_000_000, transcendentals=0),
    )(b, fb, fc, fp, ft.transpose(1, 2, 0), mb, mc.T, mp, mt.T)
    return pl.pallas_call(
        hand_over,
        out_shape=tuple(jax.ShapeDtypeStruct(o.shape, o.dtype) for o in results),
        in_specs=[any_spec] * 3,
        out_specs=(any_spec,) * 3,
        scratch_shapes=[vmem(o.shape, o.dtype) for o in results] + [dma((3, HAND)), dma((3, HAND))],
        compiler_params=pltpu.CompilerParams(vmem_limit_bytes=56 * 1024 * 1024),
    )(*results)


def solution(mesh):
    placed = (
        P("row", "grid", None, None),
        P("row", "grid", None, None, None),
        P("row", "grid", None),
        P("row", "grid", None, None, None),
        P("row", "grid", None),
        P("row", None, None, None),
        P("row", None),
        P("row", None, None, None),
        P("row", None),
    )
    return jax.shard_map(
        functools.partial(body, mesh.shape["row"], mesh.shape["grid"]),
        mesh=mesh,
        in_specs=placed,
        out_specs=(P("row", "grid", None, None), P("row", None, None), P()),
        check_vma=False,
    )
```

```python
import functools

import jax
import jax.numpy as jnp
from jax import lax
from jax.experimental import pallas as pl
from jax.experimental.pallas import tpu as pltpu
from jax.sharding import PartitionSpec as P

MESH = pl.DeviceIdType.MESH
F32 = jnp.float32
BF16 = jnp.bfloat16

C3 = 4
DEG = 3
PARTS = 2
GROUP = 4
REACH = DEG

cheb_low = 0.6
cheb_high = 6.0
CENTRE = 0.5 * (cheb_high + cheb_low)
HALF = 0.5 * (cheb_high - cheb_low)


def sweep_factors():
    ratio = CENTRE / HALF
    rho = 1.0 / ratio
    factors = []
    for _ in range(DEG - 1):
        rho_next = 1.0 / (2.0 * ratio - rho)
        factors.append((rho_next * rho, 2.0 * rho_next / HALF))
        rho = rho_next
    return factors


def copy_to(src, dst, send, recv, row, grid):
    return pltpu.make_async_remote_copy(
        src_ref=src, dst_ref=dst, send_sem=send, recv_sem=recv, device_id=(row, grid), device_id_type=MESH
    )


def kernel(
    n_row, n_grid,
    b_hbm, fb_hbm, fc, fp_hbm, ft, mb_hbm, mc, mp_hbm, mt,
    out_f, out_m, out_c,
    res, dirn, itr, fb, fp, mb, mp, halos, pieces, rs_send, rs_recv,
    m_halos, cols_send, cols_recv, edge_send, m_res, m_dir, m_itr, ag_send, ag_recv, m_turn, m_out,
    c_pair_send, c_pair_recv, c_z_send, c_z_recv, c_g_send, c_g_recv, c_all, c_turn, c_out,
    in_sem, out_sem, w_sem,
    g_send, g_recv, r_send, r_recv, k_send, k_recv,
    rs_ssem, rs_rsem, mh_send, mh_recv, mb_send, mb_recv, mc_send, mc_recv, ag_ssem, ag_rsem,
    cp_ssem, cp_rsem, cz_ssem, cz_rsem, cg_ssem, cg_rsem, ca_ssem, ca_rsem,
):
    r = lax.axis_index("row")
    g = lax.axis_index("grid")
    rx, ry = res.shape[0], res.shape[1]
    bs, loads = res.shape[2], res.shape[3]
    width = loads // PARTS
    lpd = width // n_grid
    LPD = lpd * PARTS
    n_mid = mb_hbm.shape[0]
    k2 = mb.shape[1]
    n_pair = n_row // 2
    core = lax.rem(r, 2)
    mate = r + 1 - 2 * core
    top, bottom = r == 0, r == n_row - 1
    first, last = g == 0, g == n_grid - 1
    half_c = C3 // 2

    for x in range(rx):
        pltpu.make_async_copy(b_hbm.at[x], res.at[x], in_sem.at[x]).start()
    weights = (
        pltpu.make_async_copy(fb_hbm, fb, w_sem.at[0]),
        pltpu.make_async_copy(fp_hbm, fp, w_sem.at[1]),
        pltpu.make_async_copy(mb_hbm, mb.at[pl.ds(REACH - 1, mb_hbm.shape[0])], w_sem.at[2]),
        pltpu.make_async_copy(mp_hbm, mp, w_sem.at[3]),
    )
    for w in weights:
        w.start()

    barrier = pltpu.get_barrier_semaphore()

    def greet(row, grid):
        pl.semaphore_signal(barrier, inc=1, device_id=(row, grid), device_id_type=MESH)

    @pl.loop(1, n_grid)
    def _(s):
        greet(r, lax.rem(g + s, n_grid))

    @pl.loop(1, n_pair)
    def _(s):
        greet(lax.rem(r + 2 * s, n_row), g)

    greet(mate, g)
    outer = r - 1 + 2 * core
    has_outer = jnp.logical_and(outer >= 0, outer < n_row)

    @pl.when(has_outer)
    def _():
        greet(outer, g)

    zero = jnp.zeros((bs, width), BF16)

    def clear_row(xi):
        for it in range(DEG):
            for h in range(PARTS):
                for yi in range(ry + 2):
                    halos[it][h][yi, xi] = zero

    def clear_column(yi):
        for it in range(DEG):
            for h in range(PARTS):
                for xi in range(rx + 2):
                    halos[it][h][yi, xi] = zero

    def clear_mid(side):
        for e in range(REACH):
            m_res[side * (n_mid + REACH) + e] = jnp.zeros((LPD, bs), F32)
        cols_recv[side] = jnp.zeros(cols_recv.shape[1:], BF16)
        for e in range(REACH - 1):
            for k in range(k2):
                mb[side * (n_mid + REACH - 1) + e, k] = jnp.zeros((bs, bs), BF16)

    @pl.when(top)
    def _():
        clear_row(0)
        clear_mid(0)

    @pl.when(bottom)
    def _():
        clear_row(rx + 1)
        clear_mid(1)

    @pl.when(first)
    def _():
        clear_column(0)

    @pl.when(last)
    def _():
        clear_column(ry + 1)

    def send_block(it, h, x, y):
        src = halos[it][h].at[y + 1, x + 1]
        to = g + 2 * y - 1

        @pl.when(jnp.logical_and(to >= 0, to < n_grid))
        def _():
            dst = halos[it][h].at[3 * (1 - y), x + 1]
            copy_to(src, dst, g_send.at[it, h, y, x], g_recv.at[it, h, 1 - y, x], r, to).start()

        @pl.when(jnp.logical_and(x == 0, jnp.logical_not(top)))
        def _():
            dst = halos[it][h].at[y + 1, rx + 1]
            copy_to(src, dst, r_send.at[it, h, 0, y], r_recv.at[it, h, 1, y], r - 1, g).start()

        @pl.when(jnp.logical_and(x == rx - 1, jnp.logical_not(bottom)))
        def _():
            dst = halos[it][h].at[y + 1, 0]
            copy_to(src, dst, r_send.at[it, h, 1, y], r_recv.at[it, h, 0, y], r + 1, g).start()

    def grid_block(it, h, side, x):
        block = halos[it][h].at[3 * side, x + 1]
        return copy_to(block, block, g_send.at[it, h, 1 - side, x], g_recv.at[it, h, side, x], r, g)

    def corner(it, h, up, side):
        src = halos[it][h].at[3 * side, 1 + up * (rx - 1)]
        dst = halos[it][h].at[3 * side, (rx + 1) * (1 - up)]
        return copy_to(src, dst, k_send.at[it, h, up, side], k_recv.at[it, h, 1 - up, side], r - 1 + 2 * up, g)

    def row_block(it, h, up, y):
        block = halos[it][h].at[y + 1, (rx + 1) * up]
        return copy_to(block, block, r_send.at[it, h, up, y], r_recv.at[it, h, up, y], r, g)

    def corner_in(it, h, up, side):
        block = halos[it][h].at[3 * side, (rx + 1) * up]
        return copy_to(block, block, k_send.at[it, h, up, side], k_recv.at[it, h, up, side], r, g)

    sides = ((0, jnp.logical_not(first)), (1, jnp.logical_not(last)))
    ends = ((0, jnp.logical_not(top)), (1, jnp.logical_not(bottom)))

    def forward_corners(it, h):
        for side, there in sides:
            @pl.when(there)
            def _():
                for up, on in ends:
                    grid_block(it, h, side, up * (rx - 1)).wait_recv()

                    @pl.when(on)
                    def _():
                        corner(it, h, up, side).start()

    def wait_halo(it, h):
        for side, there in sides:
            @pl.when(there)
            def _():
                for x in range(1, rx - 1):
                    grid_block(it, h, side, x).wait_recv()
        for up, on in ends:
            @pl.when(on)
            def _():
                for y in range(ry):
                    row_block(it, h, up, y).wait_recv()
                for side, there in sides:
                    @pl.when(there)
                    def _():
                        corner_in(it, h, up, side).wait_recv()

    def order(t):
        return (rx - t // ry) % rx, t % ry

    def mid_matrix(up, q):
        e, k = q // k2, q % k2
        src = mb.at[up * n_mid + (1 - up) * (REACH - 1) + e, k]
        dst = mb.at[(1 - up) * (n_mid + REACH - 1) + e, k]
        return copy_to(src, dst, mb_send.at[up, q], mb_recv.at[1 - up, q], r - 1 + 2 * up, g)

    def mid_columns(up):
        return copy_to(cols_send.at[up], cols_recv.at[1 - up], mc_send.at[up], mc_recv.at[1 - up], r - 1 + 2 * up, g)

    def mid_edge(up):
        src = edge_send.at[up]
        dst = m_res.at[pl.ds((1 - up) * (n_mid + REACH), REACH)]
        return copy_to(src, dst, mh_send.at[up], mh_recv.at[1 - up], r - 1 + 2 * up, g)

    for up in range(2):
        for e in range(REACH - 1):
            for k in range(k2):
                own = mc[k, up * (n_mid - REACH + 1) + e].astype(F32)
                cols_send[up, e, k] = jnp.full((LPD, bs), own, F32).astype(BF16)

    for x in range(rx):
        pltpu.make_async_copy(b_hbm.at[x], res.at[x], in_sem.at[x]).wait()
    for h in range(PARTS):
        cols = slice(h * width, (h + 1) * width)

        @pl.loop(0, rx * ry)
        def _(t):
            x, y = order(t)
            start = res[x, y, :, cols] * (1.0 / CENTRE)
            halos[0][h][y + 1, x + 1] = start.astype(BF16)
            if h == 0:
                @pl.when(t == 0)
                def _():
                    pl.semaphore_wait(barrier, n_grid - 1 + n_pair + jnp.where(has_outer, 1, 0))
            send_block(0, h, x, y)
            dirn[x, y, :, cols] = start

    weights[0].wait()
    weights[1].wait()
    factors = sweep_factors()
    n_pieces = pieces.shape[0]
    kp = fp.shape[2]

    for it in range(DEG):
        for h in range(PARTS):
            cols = slice(h * width, (h + 1) * width)
            if h == 0:
                forward_corners(it, h)
            wait_halo(it, h)
            phase = it * PARTS + h
            if phase == 0:
                weights[2].wait()
            for up, on in ends:
                @pl.when(on)
                def _():
                    if phase == 0:
                        mid_columns(up).start()
                    for q in range(phase, (REACH - 1) * k2, DEG * PARTS):
                        mid_matrix(up, q).start()

            def products(x, y):
                total = None
                for k in range(fb.shape[2]):
                    c = fc[x, y, k]
                    cx = lax.shift_right_logical(c * 11, 5)
                    picked = halos[it][h][y + c - 3 * cx, x + cx]
                    term = jnp.dot(fb[x, y, k], picked, preferred_element_type=F32)
                    total = term if total is None else total + term
                return total

            def update(x, y, total):
                left = res[x, y, :, cols] - total
                if it < DEG - 1:
                    res[x, y, :, cols] = left
                    alpha, beta = factors[it]
                    old = dirn[x, y, :, cols]
                    new = alpha * old + beta * left
                    halos[it + 1][h][y + 1, x + 1] = new.astype(BF16)
                    if it == 0:
                        dirn[x, y, :, cols] = new
                        itr[x, y, :, cols] = old + new
                    else:
                        itr[x, y, :, cols] = itr[x, y, :, cols] + new
                else:
                    turned = left.astype(BF16).T
                    for k in range(kp):
                        pieces[(x * ry + y) * kp + k] = jnp.dot(turned, fp[x, y, k], preferred_element_type=F32)

            def several(blocks):
                totals = [products(x, y) for x, y in blocks]
                for (x, y), total in zip(blocks, totals):
                    update(x, y, total)
                if it < DEG - 1:
                    for x, y in blocks:
                        send_block(it + 1, h, x, y)

            if GROUP == rx * ry:
                several([order(t) for t in range(rx * ry)])
            else:
                @pl.loop(0, rx * ry // GROUP)
                def _(t):
                    several([order(t * GROUP + u) for u in range(GROUP)])
                    if h + 1 < PARTS:
                        @pl.when(t == 0)
                        def _():
                            forward_corners(it, h + 1)

            if it == DEG - 2 and h == PARTS - 1:
                pltpu.make_async_copy(itr, out_f, out_sem.at[0]).start()

            if it == DEG - 1:
                def one_share(to):
                    rows = pl.ds(pl.multiple_of(to * lpd, lpd), lpd)
                    sums = [None] * n_mid
                    for p in range(n_pieces):
                        piece = pieces[p, rows, :]
                        target = ft[p // kp % ry, p % kp, p // kp // ry]
                        for m in range(n_mid):
                            part = jnp.where(target == m, piece, 0.0)
                            sums[m] = part if p == 0 else sums[m] + part
                    pairs = [jnp.concatenate(sums[m:m + 2], axis=1) for m in range(0, n_mid, 2)]
                    return jnp.concatenate(pairs, axis=0).astype(BF16)

                @pl.loop(0, n_grid // 2)
                def _(q):
                    near = [(2 * q + u + 1, lax.rem(g + 2 * q + u + 1, n_grid)) for u in range(2)]
                    for (_, to), share in zip(near, [one_share(to) for _, to in near]):
                        rs_send[h, to] = share
                    for s, to in near:
                        @pl.when(s < n_grid)
                        def _():
                            copy_to(
                                rs_send.at[h, to], rs_recv.at[h, g], rs_ssem.at[h, s], rs_rsem.at[h, g], r, to
                            ).start()

    for h in range(PARTS):
        def take(s, total):
            src = lax.rem(g + n_grid - s, n_grid)
            copy_to(rs_send.at[h, src], rs_recv.at[h, src], rs_ssem.at[h, s], rs_rsem.at[h, src], r, src).wait_recv()
            return total + rs_recv[h, src].astype(F32)

        total = lax.fori_loop(1, n_grid, take, rs_send[h, g].astype(F32))
        for m in range(n_mid):
            half = total[m // 2 * lpd:(m // 2 + 1) * lpd, m % 2 * bs:(m % 2 + 1) * bs]
            m_res[REACH + m, h * lpd:(h + 1) * lpd, :] = half

    for up, on in ends:
        @pl.when(on)
        def _():
            edge_send[up] = m_res[up * n_mid + (1 - up) * REACH:up * n_mid + (1 - up) * REACH + REACH]
            mid_edge(up).start()
    weights[3].wait()
    for up, on in ends:
        @pl.when(on)
        def _():
            mid_columns(1 - up).wait_recv()
            for q in range((REACH - 1) * k2):
                mid_matrix(1 - up, q).wait_recv()
            mid_edge(1 - up).wait_recv()

    start = m_res[...] * (1.0 / CENTRE)
    m_dir[...] = start
    m_halos[0][...] = start.astype(BF16)

    nt = (((1,), (1,)), ((), ()))
    kp2 = mp.shape[1]
    for it in range(DEG):
        def mid_products(e):
            total = None
            for k in range(k2):
                if REACH <= e < REACH + n_mid:
                    picked = m_halos[it][e - 1 + mc[k, e - REACH]]
                else:
                    side = int(e >= REACH)
                    where = cols_recv[side, e - 1 - side * (n_mid + REACH - 1), k].astype(F32)
                    near = [m_halos[it][e + d].astype(F32) for d in (-1, 0, 1)]
                    picked = jnp.where(where == 0.0, near[0], jnp.where(where == 1.0, near[1], near[2])).astype(BF16)
                term = lax.dot_general(picked, mb[e - 1, k], nt, preferred_element_type=F32)
                total = term if total is None else total + term
            return total

        def mid_update(e, total):
            left = m_res[e] - total
            m_res[e] = left
            if it < DEG - 1:
                alpha, beta = factors[it]
                old = m_dir[e]
                new = alpha * old + beta * left
                m_dir[e] = new
                m_halos[it + 1][e] = new.astype(BF16)
                if REACH <= e < REACH + n_mid:
                    i = e - REACH
                    m_itr[i] = old + new if it == 0 else m_itr[i] + new

        rows = range(it + 1, n_mid + 2 * REACH - 1 - it)
        totals = [mid_products(e) for e in rows]
        for e, total in zip(rows, totals):
            mid_update(e, total)

        if it == DEG - 2:
            for q in range(n_mid // 2):
                ag_send[q] = jnp.concatenate([m_itr[2 * q], m_itr[2 * q + 1]], axis=1).astype(BF16)
            ag_recv[g] = ag_send[...]

            @pl.loop(1, n_grid)
            def _(s):
                to = lax.rem(g + s, n_grid)
                copy_to(ag_send, ag_recv.at[g], ag_ssem.at[s], ag_rsem.at[g], r, to).start()

    sums = [None] * C3
    for i in range(n_mid):
        rounded = m_res[REACH + i].astype(BF16)
        for k in range(kp2):
            piece = jnp.dot(rounded, mp[i, k], preferred_element_type=F32)
            for m in range(C3):
                part = jnp.where(mt[k, i] == m, piece, 0.0)
                sums[m] = part if sums[m] is None else sums[m] + part
    low = jnp.concatenate(sums[:half_c], axis=1)
    high = jnp.concatenate(sums[half_c:], axis=1)
    mine = jnp.where(core == 0, low, high)
    c_pair_send[...] = jnp.where(core == 0, high, low).astype(BF16)
    swap = copy_to(c_pair_send, c_pair_recv, cp_ssem.at[0], cp_rsem.at[0], mate, g)
    swap.start()
    swap.wait()
    mine = mine + c_pair_recv[...].astype(F32)
    c_z_send[...] = mine.astype(BF16)

    @pl.loop(1, n_pair)
    def _(s):
        copy_to(c_z_send, c_z_recv.at[s], cz_ssem.at[s], cz_rsem.at[s], lax.rem(r + 2 * s, n_row), g).start()

    def take_z(s, total):
        copy_to(c_z_send, c_z_recv.at[s], cz_ssem.at[s], cz_rsem.at[s], r, g).wait_recv()
        return total + c_z_recv[s].astype(F32)

    mine = lax.fori_loop(1, n_pair, take_z, mine)
    c_g_send[...] = mine.astype(BF16)

    @pl.loop(1, n_grid)
    def _(s):
        to = lax.rem(g + s, n_grid)
        copy_to(c_g_send, c_g_recv.at[g], cg_ssem.at[s], cg_rsem.at[g], r, to).start()

    c_g_recv[g] = c_g_send[...]
    copy_to(c_g_recv.at[g], c_all.at[g], ca_ssem.at[g], ca_rsem.at[g], mate, g).start()

    @pl.loop(1, n_grid)
    def _(s):
        src = lax.rem(g + n_grid - s, n_grid)
        copy_to(ag_send, ag_recv.at[src], ag_ssem.at[s], ag_rsem.at[src], r, g).wait_recv()

    def spread(turn, src, block):
        wide = block.astype(F32)
        for h in range(PARTS):
            rows = pl.ds(pl.multiple_of(h * width + src * lpd, lpd), lpd)
            turn[rows, :] = wide[h * lpd:(h + 1) * lpd]

    @pl.loop(0, n_mid // 2)
    def _(q):
        for src in range(n_grid):
            spread(m_turn, src, ag_recv[src, q])
        turned = m_turn[...].T
        m_out[2 * q] = turned[:bs]
        m_out[2 * q + 1] = turned[bs:]

    pltpu.make_async_copy(m_out, out_m, out_sem.at[1]).start()

    @pl.loop(1, n_grid)
    def _(s):
        src = lax.rem(g + n_grid - s, n_grid)
        copy_to(c_g_send, c_g_recv.at[src], cg_ssem.at[s], cg_rsem.at[src], r, g).wait_recv()
        copy_to(c_g_recv.at[src], c_all.at[src], ca_ssem.at[src], ca_rsem.at[src], mate, g).start()

    @pl.loop(0, n_grid)
    def _(src):
        copy_to(c_g_recv.at[src], c_all.at[src], ca_ssem.at[src], ca_rsem.at[src], mate, g).wait_recv()

    for other in range(2):
        source = c_all if other else c_g_recv
        for src in range(n_grid):
            spread(c_turn, src, source[src])
        turned = c_turn[...].T
        for m in range(half_c):
            place = m + half_c * (other + core - 2 * other * core)
            c_out[place] = turned[m * bs:(m + 1) * bs]

    pltpu.make_async_copy(c_out, out_c, out_sem.at[2]).start()

    for up, on in ends:
        @pl.when(on)
        def _():
            mid_columns(up).wait_send()
            mid_edge(up).wait_send()
            for q in range((REACH - 1) * k2):
                mid_matrix(up, q).wait_send()

    for it in range(DEG):
        for h in range(PARTS):
            for y in range(ry):
                to = g + 2 * y - 1

                @pl.when(jnp.logical_and(to >= 0, to < n_grid))
                def _():
                    for x in range(rx):
                        grid_block(it, h, 1 - y, x).wait_send()

            for up, on in ends:
                @pl.when(on)
                def _():
                    for y in range(ry):
                        row_block(it, h, up, y).wait_send()
                    for side, there in sides:
                        @pl.when(there)
                        def _():
                            corner(it, h, up, side).wait_send()

    @pl.loop(1, n_grid)
    def _(s):
        to = lax.rem(g + s, n_grid)
        for h in range(PARTS):
            copy_to(rs_send.at[h, to], rs_recv.at[h, g], rs_ssem.at[h, s], rs_rsem.at[h, g], r, to).wait_send()
        copy_to(ag_send, ag_recv.at[g], ag_ssem.at[s], ag_rsem.at[g], r, to).wait_send()
        copy_to(c_g_send, c_g_recv.at[g], cg_ssem.at[s], cg_rsem.at[g], r, to).wait_send()

    @pl.loop(1, n_pair)
    def _(s):
        copy_to(c_z_send, c_z_recv.at[s], cz_ssem.at[s], cz_rsem.at[s], lax.rem(r + 2 * s, n_row), g).wait_send()

    @pl.loop(0, n_grid)
    def _(src):
        copy_to(c_g_recv.at[src], c_all.at[src], ca_ssem.at[src], ca_rsem.at[src], mate, g).wait_send()

    pltpu.make_async_copy(itr, out_f, out_sem.at[0]).wait()
    pltpu.make_async_copy(m_out, out_m, out_sem.at[1]).wait()
    pltpu.make_async_copy(c_out, out_c, out_sem.at[2]).wait()


HAND = 4


def hand_over(f, m, c, out_f, out_m, out_c, hold_f, hold_m, hold_c, sem_in, sem_out):
    arriving, leaving = [], []
    for n, (src, hold, dst) in enumerate(((f, hold_f, out_f), (m, hold_m, out_m), (c, hold_c, out_c))):
        part = src.shape[0] // HAND
        for q in range(HAND):
            rows = pl.ds(q * part, part)
            arriving.append(pltpu.make_async_copy(src.at[rows], hold.at[rows], sem_in.at[n, q]))
            leaving.append(pltpu.make_async_copy(hold.at[rows], dst.at[rows], sem_out.at[n, q]))
    for copy in arriving:
        copy.start()
    for came, goes in zip(arriving, leaving):
        came.wait()
        goes.start()
    for copy in leaving:
        copy.wait()


def body(n_row, n_grid, b, fb, fc, fp, ft, mb, mc, mp, mt):
    rx, ry, bs, loads = b.shape
    width = loads // PARTS
    lpd = width // n_grid
    LPD = lpd * PARTS
    n_mid = mb.shape[0]
    kp = fp.shape[2]
    half_c = C3 // 2
    any_spec = pl.BlockSpec(memory_space=pl.ANY)
    smem = pl.BlockSpec(memory_space=pltpu.SMEM)
    vmem = pltpu.VMEM
    dma = pltpu.SemaphoreType.DMA
    flops = 2 * bs * bs * loads * rx * ry * (fb.shape[2] * DEG + kp)
    results = pl.pallas_call(
        functools.partial(kernel, n_row, n_grid),
        out_shape=(
            jax.ShapeDtypeStruct(b.shape, F32),
            jax.ShapeDtypeStruct((n_mid, bs, loads), F32),
            jax.ShapeDtypeStruct((C3, bs, loads), F32),
        ),
        in_specs=[any_spec, any_spec, smem, any_spec, smem, any_spec, smem, any_spec, smem],
        out_specs=(any_spec, any_spec, any_spec),
        scratch_shapes=[
            vmem(b.shape, F32),
            vmem(b.shape, F32),
            vmem(b.shape, F32),
            vmem(fb.shape, BF16),
            vmem(fp.shape, BF16),
            vmem((n_mid + 2 * REACH - 2,) + mb.shape[1:], BF16),
            vmem(mp.shape, BF16),
            [[vmem((ry + 2, rx + 2, bs, width), BF16)] * PARTS] * DEG,
            vmem((rx * ry * kp, width, bs), F32),
            vmem((PARTS, n_grid, n_mid // 2 * lpd, 2 * bs), BF16),
            vmem((PARTS, n_grid, n_mid // 2 * lpd, 2 * bs), BF16),
            [vmem((n_mid + 2 * REACH, LPD, bs), BF16)] * DEG,
            vmem((2, REACH - 1, mb.shape[1], LPD, bs), BF16),
            vmem((2, REACH - 1, mb.shape[1], LPD, bs), BF16),
            vmem((2, REACH, LPD, bs), F32),
            vmem((n_mid + 2 * REACH, LPD, bs), F32),
            vmem((n_mid + 2 * REACH, LPD, bs), F32),
            vmem((n_mid, LPD, bs), F32),
            vmem((n_mid // 2, LPD, 2 * bs), BF16),
            vmem((n_grid, n_mid // 2, LPD, 2 * bs), BF16),
            vmem((loads, 2 * bs), F32),
            vmem((n_mid, bs, loads), F32),
            vmem((LPD, half_c * bs), BF16),
            vmem((LPD, half_c * bs), BF16),
            vmem((LPD, half_c * bs), BF16),
            vmem((n_row // 2, LPD, half_c * bs), BF16),
            vmem((LPD, half_c * bs), BF16),
            vmem((n_grid, LPD, half_c * bs), BF16),
            vmem((n_grid, LPD, half_c * bs), BF16),
            vmem((loads, half_c * bs), F32),
            vmem((C3, bs, loads), F32),
            dma((rx,)), dma((3,)), dma((4,)),
            dma((DEG, PARTS, 2, rx)), dma((DEG, PARTS, 2, rx)),
            dma((DEG, PARTS, 2, ry)), dma((DEG, PARTS, 2, ry)),
            dma((DEG, PARTS, 2, 2)), dma((DEG, PARTS, 2, 2)),
            dma((PARTS, n_grid)), dma((PARTS, n_grid)),
            dma((2,)), dma((2,)),
            dma((2, (REACH - 1) * mb.shape[1])), dma((2, (REACH - 1) * mb.shape[1])),
            dma((2,)), dma((2,)),
            dma((n_grid,)), dma((n_grid,)),
            dma((1,)), dma((1,)),
            dma((n_row // 2,)), dma((n_row // 2,)),
            dma((n_grid,)), dma((n_grid,)),
            dma((n_grid,)), dma((n_grid,)),
        ],
        compiler_params=pltpu.CompilerParams(
            collective_id=0, has_side_effects=True, vmem_limit_bytes=56 * 1024 * 1024
        ),
        cost_estimate=pl.CostEstimate(flops=flops, bytes_accessed=13_000_000, transcendentals=0),
    )(b, fb, fc, fp, ft.transpose(1, 2, 0), mb, mc.T, mp, mt.T)
    return pl.pallas_call(
        hand_over,
        out_shape=tuple(jax.ShapeDtypeStruct(o.shape, o.dtype) for o in results),
        in_specs=[any_spec] * 3,
        out_specs=(any_spec,) * 3,
        scratch_shapes=[vmem(o.shape, o.dtype) for o in results] + [dma((3, HAND)), dma((3, HAND))],
        compiler_params=pltpu.CompilerParams(vmem_limit_bytes=56 * 1024 * 1024),
    )(*results)


def solution(mesh):
    placed = (
        P("row", "grid", None, None),
        P("row", "grid", None, None, None),
        P("row", "grid", None),
        P("row", "grid", None, None, None),
        P("row", "grid", None),
        P("row", None, None, None),
        P("row", None),
        P("row", None, None, None),
        P("row", None),
    )
    return jax.shard_map(
        functools.partial(body, mesh.shape["row"], mesh.shape["grid"]),
        mesh=mesh,
        in_specs=placed,
        out_specs=(P("row", "grid", None, None), P("row", None, None), P()),
        check_vma=False,
    )
```
